512 devices in a mesh: lists: 128 (over y, z, core), rep: 4 (over x).
Axes of the slice: x: 4, y: 8, z: 8, core: 2. Of those that a mesh axis runs over, the one named last changes fastest.
Arguments:
- vector_codes: bfloat16 [65536, 1024], P(('lists', 'rep')), may hold values from -6 to 6
- row_scales: bfloat16 [65536], P(('lists', 'rep')), may hold values from 0.29882812 to 3
- old_list: int32 [65536], P(('lists', 'rep')), may hold values from 0 to 65535, as said below
- new_list: int32 [65536], P(('lists', 'rep')), may hold values from 0 to 65535, as said below
- pq_codes: int32 [65536, 64], P(('lists', 'rep')), may hold values from 0 to 255
- centroids: bfloat16 [65536, 1024], P('lists'), may hold values from -6 to 6
Outputs:
- centroid_delta: bfloat16 [65536, 1024], P('lists', 'rep')
- codebook_sums: float32 [64, 4096], P('rep')
The draws below stay inside these ranges and needn't reach their ends.
Inputs may be any that keep to these rules, and one draw needn't show every extreme that they name: `old_list`: every row held by the device at lists index i names a list from i * 512 to (i + 1) * 512 - 1. `new_list`: the owner of list l is lists index l // 512. Among the rows of one device at most 2 name lists of one owner, and in every draw one owner is named by exactly 2 rows of every device.
All inputs are finite; a program needn't handle non-finite values.
Results may differ from the reference program's by a relative error of at most 0.009.
Values may be sent and summed in bfloat16 or wider, within the bound.
A program may use at most 64 MiB of HBM per device.

```python
import math
import jax
import jax.numpy as jnp

D = 1024
M = 64
KSUB = 256
LIST_DEV = 512
VEC_DEV = 128
CAP = 2
NLIST = 65536
VECS = 65536
N_LISTS = 128
N_REP = 4


def draw_new_list(key, part):
    key = jax.random.fold_in(key, 11)
    block_total = N_LISTS * N_REP
    slot_count = N_LISTS * CAP
    hot_owner = jax.random.randint(jax.random.fold_in(key, 1), (), 0, N_LISTS)

    def one_block(block_index):
        block_key = jax.random.fold_in(key, block_index + 2)
        first_key, second_key, third_key = jax.random.split(block_key, 3)
        shuffled = jax.random.permutation(first_key, slot_count).astype(jnp.int32)
        slot_ids = jnp.arange(slot_count, dtype=jnp.int32)
        ranking = jnp.where(slot_ids // CAP == hot_owner, 0, slot_count) + shuffled
        chosen = jnp.argsort(ranking)[:VEC_DEV].astype(jnp.int32)
        chosen = chosen[jax.random.permutation(second_key, VEC_DEV)]
        owners = chosen // CAP
        inside = jax.random.randint(third_key, (VEC_DEV,), 0, LIST_DEV)
        return (owners * LIST_DEV + inside).astype(jnp.int32)
    return jax.vmap(one_block)(jnp.arange(block_total, dtype=jnp.int32)).reshape(-1)


def draw_old_list(key, part):
    key = jax.random.fold_in(key, 23)
    row_total = N_LISTS * N_REP * VEC_DEV
    block_ids = jnp.arange(row_total, dtype=jnp.int32) // VEC_DEV
    owners = block_ids // N_REP
    inside = jax.random.randint(key, (row_total,), 0, LIST_DEV)
    return (owners * LIST_DEV + inside).astype(jnp.int32)


def touch_ends(entries, rng, least, largest):
    place = [jax.random.randint(jax.random.fold_in(rng, axis), (), 0, length) for axis, length in enumerate(entries.shape)]
    widest = entries.shape.index(max(entries.shape))
    beside = place[:widest] + [(place[widest] + 1) % entries.shape[widest]] + place[widest + 1:]
    return entries.at[tuple(place)].set(least).at[tuple(beside)].set(largest)


def levels(stream_key, dims, cuts, smallest, high):
    factor_of = 1.0
    for dim, shards_of in cuts:
        steps = jax.random.uniform(jax.random.fold_in(jax.random.fold_in(stream_key, 6), dim), (shards_of,), jnp.float32, smallest / len(cuts), high / len(cuts))
        factor_of = factor_of * jnp.repeat(jnp.exp(steps), dims[dim] // shards_of).reshape((-1,) + (1,) * (len(dims) - 1 - dim))
    return factor_of


def noise(rng, extent, spread, reach, shards=(), held_as=jnp.bfloat16):
    loudness = levels(rng, extent, shards, -0.22, 0.18) if shards else 1.0
    entries = jax.random.normal(rng, extent, jnp.float32) * spread * loudness
    return jnp.minimum(jnp.maximum(entries, -reach), reach).astype(held_as)


def setup_inputs(seed: int = 0) -> dict:
    seeds = jax.random.split(jax.random.key(seed), 7)
    vector_codes = noise(seeds[0], (VECS, D), 1.0, 6.0, ((0, 512),))
    row_scales = jnp.clip(jnp.exp(math.log(3.0) - 2.306499 * jax.random.uniform(seeds[1], (VECS,), jnp.float32) ** levels(seeds[1], (VECS,), ((0, 512),), -0.2, 0.2)), 0.29882812, 3.0).astype(jnp.bfloat16)
    old_list = draw_old_list(jax.random.fold_in(seeds[6], 71), 0)
    new_list = draw_new_list(jax.random.fold_in(seeds[6], 71), 0)
    pq_codes = touch_ends(jax.random.randint(seeds[4], (VECS, M), 0, KSUB), jax.random.fold_in(seeds[4], 1), 0, KSUB - 1).astype(jnp.int32)
    centroids = noise(seeds[5], (NLIST, D), 1.0, 6.0, ((0, 128),))
    return dict(vector_codes=vector_codes, row_scales=row_scales, old_list=old_list, new_list=new_list, pq_codes=pq_codes, centroids=centroids)


def reference(vector_codes, row_scales, old_list, new_list, pq_codes, centroids):
    values = vector_codes.astype(jnp.float32) * row_scales.astype(jnp.float32)[:, None]
    total_lists = centroids.shape[0]
    new_sum = jax.ops.segment_sum(values, new_list, num_segments=total_lists)
    old_sum = jax.ops.segment_sum(values, old_list, num_segments=total_lists)
    centroid_delta = (new_sum - old_sum).astype(jnp.bfloat16)
    nearest = jnp.take(centroids, new_list, axis=0).astype(jnp.float32)
    residual = (values - nearest).astype(jnp.bfloat16)
    sub_width = residual.shape[1] // M
    pieces = residual.astype(jnp.float32).reshape(-1, sub_width)
    labels = (pq_codes + (jnp.arange(M, dtype=jnp.int32) * KSUB)[None, :]).reshape(-1)
    sums = jax.ops.segment_sum(pieces, labels, num_segments=M * KSUB)
    return centroid_delta, sums.reshape(M, KSUB * sub_width)
```

```python
import functools

import jax
import jax.numpy as jnp
from jax import lax
from jax.experimental import pallas as pl
from jax.experimental.pallas import tpu as pltpu
from jax.sharding import PartitionSpec as P

MESH = pl.DeviceIdType.MESH
F32 = jnp.float32
BF16 = jnp.bfloat16
I32 = jnp.int32

N_LISTS = 128
N_REP = 4
CHIPS = N_LISTS // 2
ROWS = 128
GROUP = ROWS * N_REP
LISTS = 512
COLS = 256
SLOTS = 8
KK = 16
KSUB = 256
NT = (((1,), (1,)), ((), ()))
NN = (((1,), (0,)), ((), ()))


def dot(a, b, dims=NN):
    return lax.dot_general(a, b, dims, preferred_element_type=F32)


def iota(shape, axis):
    return lax.broadcasted_iota(I32, shape, axis)


def chip_at(chip, step):
    off = lax.rem(step * 27, CHIPS)
    y = lax.rem(chip // 8 + off // 8, 8)
    z = lax.rem(lax.rem(chip, 8) + lax.rem(off, 8), 8)
    return y * 8 + z


def list_peer(me, step):
    off = lax.rem(step * 53, N_LISTS)
    y = lax.rem(me // 16 + off // 16, 8)
    z = lax.rem(lax.rem(me // 2, 8) + lax.rem(off // 2, 8), 8)
    c = lax.rem(lax.rem(me, 2) + lax.rem(off, 2), 2)
    return (y * 8 + z) * 2 + c


def kernel(
    codes,
    scale_ref,
    old_ref,
    new_ref,
    pq_ref,
    cent_hbm,
    delta_out,
    book_out,
    cent,
    xbuf,
    msend,
    mrecv,
    esend,
    erecv,
    vsend,
    vrecv,
    delta_acc,
    vflat,
    pqk,
    centg,
    book,
    sib,
    comb,
    rsbuf,
    tile,
    gathered,
    cent_sem,
    loc_sem,
    xs_sem,
    xr_sem,
    ms_sem,
    mr_sem,
    es_sem,
    er_sem,
    vs_sem,
    vr_sem,
    bs_sem,
    br_sem,
    rs_sem,
    rr_sem,
    ts_sem,
    tr_sem,
    gs_sem,
    gr_sem,
):
    me = lax.axis_index("lists")
    rep = lax.axis_index("rep")
    core = lax.rem(me, 2)
    chip = me // 2
    sibling = me + 1 - 2 * core

    def copy_to(src, dst, ssem, rsem, **device):
        return pltpu.make_async_remote_copy(
            src, dst, ssem, rsem, device_id=device, device_id_type=MESH
        )

    cent_copy = pltpu.make_async_copy(
        cent_hbm.at[:, pl.ds(pl.multiple_of(rep * COLS, COLS), COLS)], cent, cent_sem
    )
    cent_copy.start()

    barrier = pltpu.get_barrier_semaphore()
    for k in range(1, N_REP):
        pl.semaphore_signal(
            barrier, inc=1, device_id={"rep": lax.rem(rep + k, N_REP)}, device_id_type=MESH
        )

    def greet(k, carry):
        pl.semaphore_signal(
            barrier, inc=1, device_id={"lists": list_peer(me, k)}, device_id_type=MESH
        )
        return carry

    lax.fori_loop(1, N_LISTS, greet, 0)

    scale = scale_ref[...].astype(F32)
    new = new_ref[...]
    owner = new // LISTS
    new_in = new - owner * LISTS + 1
    old_in = old_ref[...] - me * LISTS
    own_row = jnp.broadcast_to(owner.astype(F32), (ROWS, ROWS))
    own_col = jnp.transpose(own_row)
    earlier = (own_row == own_col) & (iota((ROWS, ROWS), 0) < iota((ROWS, ROWS), 1))
    rank = jnp.sum(jnp.where(earlier, 1.0, 0.0), axis=0, keepdims=True)
    target = owner.astype(F32) * 2.0 + rank
    new_hi = new_in // 256
    old_hi = old_in // 256
    shape = (N_REP * 32, 64)
    line = iota(shape, 0)
    pick = (line // 32) * 16 + 2 * lax.rem(line, 16) + lax.rem(line, 32) // 16
    pick = jnp.where(lax.rem(line, 16) < 8, pick, -1)
    chooser = jnp.where(pick == iota(shape, 1), 1.0, 0.0).astype(BF16)
    meta = dot(chooser, pq_ref[...].astype(F32).astype(BF16), NT)
    line = lax.rem(iota((N_REP * 32, ROWS), 0), 32)
    extra = (
        (8, (new_in - new_hi * 256).astype(F32)),
        (24, new_hi.astype(F32)),
        (9, scale),
        (10, target),
        (11, (old_in - old_hi * 256).astype(F32)),
        (27, old_hi.astype(F32)),
    )
    for at, row in extra:
        meta = jnp.where(line == at, row, meta)
    msend[...] = meta.astype(BF16).reshape(N_REP, 32, ROWS)

    pl.semaphore_wait(barrier, N_LISTS - 1 + N_REP - 1)

    for k in range(1, N_REP):
        peer = lax.rem(rep + k, N_REP)
        copy_to(msend.at[peer], mrecv.at[rep], ms_sem, mr_sem, rep=peer).start()
    for k in range(1, N_REP):
        peer = lax.rem(rep + k, N_REP)
        copy_to(
            codes.at[:, pl.ds(pl.multiple_of(peer * COLS, COLS), COLS)],
            xbuf.at[rep],
            xs_sem,
            xr_sem,
            rep=peer,
        ).start()
    own = pltpu.make_async_copy(
        codes.at[:, pl.ds(pl.multiple_of(rep * COLS, COLS), COLS)], xbuf.at[rep], loc_sem
    )
    own.start()
    mrecv[rep] = msend[rep]
    peer = lax.rem(rep + 1, N_REP)
    three = mrecv.at[pl.ds(0, N_REP - 1)]
    wait = copy_to(three, three, ms_sem, mr_sem, rep=peer)
    wait.wait_recv()
    wait.wait_send()

    low = jnp.concatenate([mrecv[s, 0:16, :] for s in range(N_REP)], axis=1).astype(F32)
    high = jnp.concatenate([mrecv[s, 16:32, :] for s in range(N_REP)], axis=1).astype(F32)
    target = low[10:11, :].astype(I32)
    owner = target // 2
    slot = (iota((1, GROUP), 1) // ROWS) * 2 + target - owner * 2
    at_owner = jnp.where(iota((N_LISTS, GROUP), 0) == owner, 1.0, 0.0).astype(BF16)
    slot_b = jnp.broadcast_to(slot, (KK, GROUP))
    low_s = jnp.concatenate([jnp.where(slot_b == q, low, 0.0) for q in range(SLOTS)], axis=0)
    high_s = jnp.concatenate([jnp.where(slot_b == q, high, 0.0) for q in range(SLOTS)], axis=0)
    routed = dot(at_owner, low_s.astype(BF16), NT) + 256.0 * dot(
        at_owner, high_s.astype(BF16), NT
    )
    esend[...] = routed.reshape(N_LISTS, 1, SLOTS * KK)

    def send_meta(k, carry):
        peer = list_peer(me, k)
        copy_to(esend.at[peer], erecv.at[me], es_sem, er_sem, lists=peer).start()
        return carry

    lax.fori_loop(1, N_LISTS, send_meta, 0)
    erecv[me] = esend[me]

    own.wait()
    three = xbuf.at[pl.ds(0, N_REP - 1)]
    wait = copy_to(three, three, xs_sem, xr_sem, rep=peer)
    wait.wait_recv()
    wait.wait_send()
    place = owner * SLOTS + slot
    x = xbuf[...].reshape(GROUP, COLS)
    move = jnp.where(iota((N_LISTS * SLOTS, GROUP), 0) == place, 1.0, 0.0).astype(BF16)
    moved = dot(move, x).reshape(N_LISTS, SLOTS, COLS)
    vsend[...] = jnp.concatenate([moved[:, :, 0:128], moved[:, :, 128:256]], axis=1).astype(BF16)

    def send_vec(k, carry):
        peer = list_peer(me, k)
        copy_to(vsend.at[peer], vrecv.at[me], vs_sem, vr_sem, lists=peer).start()
        return carry

    lax.fori_loop(1, N_LISTS, send_vec, 0)
    vrecv[me] = vsend[me]

    scale = low[9:10, :]
    old_in = low[11:12, :] + 256.0 * high[11:12, :]
    weight = jnp.where(iota((LISTS, GROUP), 0).astype(F32) == old_in, scale, 0.0).astype(BF16)
    delta_acc[...] = dot(weight, x)
    pqk[0:8, 0:GROUP] = low[0:8, :]
    pqk[8:16, 0:GROUP] = high[0:8, :]
    code = iota((KSUB, GROUP), 0).astype(F32)
    lane_sub = iota((KSUB, 128), 1) // 16

    def value_sums(i, carry):
        sub = 2 * lax.rem(i, 8) + i // 8
        half = sub // 8
        hits = jnp.where(code == pqk[pl.ds(i, 1), 0:GROUP], scale, 0.0).astype(BF16)
        cols = xbuf[:, :, pl.ds(pl.multiple_of(half * 128, 128), 128)].reshape(GROUP, 128)
        total = dot(hits, cols)
        at = pl.ds(pl.multiple_of(half * KSUB, KSUB), KSUB)
        book[at, :] = jnp.where(lane_sub == lax.rem(sub, 8), total, book[at, :])
        return carry

    book[...] = jnp.zeros_like(book)
    lax.fori_loop(0, 16, value_sums, 0)

    cent_copy.wait()
    eye = jnp.where(iota((COLS, COLS), 0) == iota((COLS, COLS), 1), 1.0, 0.0).astype(BF16)
    cent_t = dot(eye, cent[...], NT).astype(BF16)

    most = erecv.at[pl.ds(0, N_LISTS - 1)]
    wait = copy_to(most, most, es_sem, er_sem, lists=sibling)
    wait.wait_recv()
    wait.wait_send()
    got = jnp.transpose(erecv[...].reshape(N_LISTS, SLOTS * KK))
    new_rows = []
    scale_rows = []
    for q in range(SLOTS):
        pairs = got[q * KK : q * KK + 8, :]
        odd = jnp.floor(pairs * (1.0 / 256.0))
        pqk[0:8, q * 128 : (q + 1) * 128] = pairs - 256.0 * odd
        pqk[8:16, q * 128 : (q + 1) * 128] = odd
        new_rows.append(got[q * KK + 8 : q * KK + 9, :])
        scale_rows.append(got[q * KK + 9 : q * KK + 10, :])
    new_in = jnp.concatenate(new_rows, axis=1) - 1.0
    new_scale = jnp.concatenate(scale_rows, axis=1)
    inside = iota((LISTS, N_LISTS * SLOTS), 0).astype(F32) == new_in
    centg[...] = dot(cent_t, jnp.where(inside, 1.0, 0.0).astype(BF16)).astype(BF16)
    code = iota((KSUB, N_LISTS * SLOTS), 0).astype(F32)

    def cent_sums(i, carry):
        sub = 2 * lax.rem(i, 8) + i // 8
        half = sub // 8
        hits = jnp.where(code == pqk[pl.ds(i, 1), :], 1.0, 0.0).astype(BF16)
        total = dot(hits, centg[pl.ds(pl.multiple_of(half * 128, 128), 128), :], NT)
        at = pl.ds(pl.multiple_of(half * KSUB, KSUB), KSUB)
        book[at, :] = book[at, :] - jnp.where(lane_sub == lax.rem(sub, 8), total, 0.0)
        return carry

    lax.fori_loop(0, 16, cent_sums, 0)
    comb[...] = book[...].reshape(CHIPS // 2, 2, 8, 128)

    pair = copy_to(comb.at[:, 1 - core], sib, bs_sem, br_sem, lists=sibling)
    pair.start()
    pair.wait()
    sib[...] = sib[...] + comb[:, core]

    def send_tile(q, carry):
        there = 2 * q + core

        @pl.when(there != chip)
        def _():
            copy_to(
                sib.at[q], rsbuf.at[chip], rs_sem, rr_sem, lists=2 * there + core
            ).start()

        return carry

    lax.fori_loop(0, CHIPS // 2, send_tile, 0)
    sums_here = lax.rem(chip, 2) == core

    @pl.when(sums_here)
    def _():
        rsbuf[chip] = sib[chip // 2]
        most = rsbuf.at[pl.ds(0, CHIPS - 1)]
        copy_to(most, most, rs_sem, rr_sem, lists=sibling).wait_recv()
        total = jnp.sum(rsbuf[...], axis=0)
        shift = lax.rem(iota((8, 128), 1) // 16 - iota((8, 128), 0) + 8, 8)
        turned = total
        for d in range(1, 8):
            moved = pltpu.roll(pltpu.roll(total, 8 - d, 0), 16 * d, 1)
            turned = jnp.where(shift == d, moved, turned)
        tile[...] = turned
        give = copy_to(tile, tile, ts_sem, tr_sem, lists=sibling)
        give.start()
        give.wait_send()
        most = sib.at[pl.ds(0, CHIPS // 2 - 1)]
        copy_to(most, most, rs_sem, rr_sem, lists=sibling).wait_send()

    @pl.when(jnp.logical_not(sums_here))
    def _():
        copy_to(tile, tile, ts_sem, tr_sem, lists=sibling).wait_recv()
        copy_to(sib, sib, rs_sem, rr_sem, lists=sibling).wait_send()

    def send_sum(k, carry):
        there = chip_at(chip, k)
        copy_to(tile, gathered.at[chip], gs_sem, gr_sem, lists=2 * there + core).start()
        return carry

    lax.fori_loop(1, CHIPS, send_sum, 0)
    gathered[chip] = tile[...]

    most = vrecv.at[pl.ds(0, N_LISTS - 1)]
    wait = copy_to(most, most, vs_sem, vr_sem, lists=sibling)
    wait.wait_recv()
    wait.wait_send()
    vflat[...] = vrecv[...].astype(F32).reshape(N_LISTS * 16, 128)
    vecs = jnp.concatenate(
        [
            jnp.concatenate(
                [vflat[pl.ds(h * 8 + q, N_LISTS, stride=16), :].astype(BF16) for h in range(2)],
                axis=1,
            )
            for q in range(SLOTS)
        ],
        axis=0,
    )
    weight = jnp.where(inside, new_scale, 0.0).astype(BF16)
    delta_out[...] = (dot(weight, vecs) - delta_acc[...]).astype(BF16)

    most = gathered.at[pl.ds(0, CHIPS - 1)]
    wait = copy_to(most, most, gs_sem, gr_sem, lists=sibling)
    wait.wait_recv()
    wait.wait_send()
    for t in range(CHIPS):
        half, block = t // 32, t % 32
        book_out[half * 8 : half * 8 + 8, block * 128 : (block + 1) * 128] = gathered[t]


def body(vector_codes, row_scales, old_list, new_list, pq_codes, centroids):
    vmem = pl.BlockSpec(memory_space=pltpu.VMEM)
    return pl.pallas_call(
        kernel,
        name="rebuild_window",
        out_shape=(
            jax.ShapeDtypeStruct((LISTS, COLS), BF16),
            jax.ShapeDtypeStruct((16, 4096), F32),
        ),
        in_specs=[vmem] * 5 + [pl.BlockSpec(memory_space=pl.ANY)],
        out_specs=(vmem, vmem),
        scratch_shapes=[
            pltpu.VMEM((LISTS, COLS), BF16),
            pltpu.VMEM((N_REP, ROWS, COLS), BF16),
            pltpu.VMEM((N_REP, 32, ROWS), BF16),
            pltpu.VMEM((N_REP, 32, ROWS), BF16),
            pltpu.VMEM((N_LISTS, 1, 128), F32),
            pltpu.VMEM((N_LISTS, 1, 128), F32),
            pltpu.VMEM((N_LISTS, 16, 128), BF16),
            pltpu.VMEM((N_LISTS, 16, 128), BF16),
            pltpu.VMEM((LISTS, COLS), F32),
            pltpu.VMEM((N_LISTS * 16, 128), F32),
            pltpu.VMEM((16, N_LISTS * SLOTS), F32),
            pltpu.VMEM((COLS, N_LISTS * SLOTS), BF16),
            pltpu.VMEM((2 * KSUB, 128), F32),
            pltpu.VMEM((CHIPS // 2, 8, 128), F32),
            pltpu.VMEM((CHIPS // 2, 2, 8, 128), F32),
            pltpu.VMEM((CHIPS, 8, 128), F32),
            pltpu.VMEM((8, 128), F32),
            pltpu.VMEM((CHIPS, 8, 128), F32),
        ]
        + [pltpu.SemaphoreType.DMA] * 18,
        compiler_params=pltpu.CompilerParams(
            collective_id=0, has_side_effects=True, vmem_limit_bytes=48 * 1024 * 1024
        ),
    )(
        vector_codes,
        row_scales.reshape(1, ROWS),
        old_list.reshape(1, ROWS),
        new_list.reshape(1, ROWS),
        pq_codes,
        centroids,
    )


def solution(mesh):
    return jax.shard_map(
        body,
        mesh=mesh,
        in_specs=(
            P(("lists", "rep"), None),
            P(("lists", "rep")),
            P(("lists", "rep")),
            P(("lists", "rep")),
            P(("lists", "rep"), None),
            P("lists", None),
        ),
        out_specs=(P("lists", "rep"), P("rep", None)),
        check_vma=False,
    )
```

```python
import functools

import jax
import jax.numpy as jnp
from jax import lax
from jax.experimental import pallas as pl
from jax.experimental.pallas import tpu as pltpu
from jax.sharding import PartitionSpec as P

MESH = pl.DeviceIdType.MESH
F32 = jnp.float32
BF16 = jnp.bfloat16
I32 = jnp.int32

N_LISTS = 128
N_REP = 4
CHIPS = N_LISTS // 2
ROWS = 128
GROUP = ROWS * N_REP
LISTS = 512
COLS = 256
SLOTS = 8
KK = 16
KSUB = 256
UNROLL = 4
NT = (((1,), (1,)), ((), ()))
NN = (((1,), (0,)), ((), ()))


def dot(a, b, dims=NN):
    return lax.dot_general(a, b, dims, preferred_element_type=F32)


def iota(shape, axis):
    return lax.broadcasted_iota(I32, shape, axis)


def wrap(value, size):
    return jnp.where(value >= size, value - size, value)


def each_peer(me, visit):
    y, z, core = me // 16 * 16, lax.rem(me // 2, 8), lax.rem(me, 2)
    places = [2 * wrap(z + i // 2, 8) + wrap(core + i % 2, 2) for i in range(16)]

    def step(t, carry):
        start = wrap(y + 16 * t, N_LISTS)
        for i in range(16):
            peer = wrap(start + 16 * (3 * (i // 2) % 8), N_LISTS) + places[i]
            if i == 0:

                @pl.when(t > 0)
                def _():
                    visit(peer)
            else:
                visit(peer)
        return carry

    lax.fori_loop(0, 8, step, 0)


def each_chip(chip, visit):
    y, z = chip // 8 * 8, lax.rem(chip, 8)
    places = [wrap(z + i, 8) for i in range(8)]

    def step(t, carry):
        start = wrap(y + 8 * t, CHIPS)
        for i in range(8):
            there = wrap(start + 8 * (3 * i % 8), CHIPS) + places[i]
            if i == 0:

                @pl.when(t > 0)
                def _():
                    visit(there)
            else:
                visit(there)
        return carry

    lax.fori_loop(0, 8, step, 0)


def kernel(
    codes_hbm,
    scale_ref,
    old_ref,
    new_ref,
    pq_hbm,
    cent_hbm,
    delta_out,
    book_out,
    pq,
    cent,
    xbuf,
    msend,
    mrecv,
    esend,
    erecv,
    vsend,
    vrecv,
    delta_acc,
    vflat,
    pqk,
    centg,
    book,
    sib,
    comb,
    rsbuf,
    tile,
    gathered,
    pq_sem,
    cent_sem,
    loc_sem,
    xs_sem,
    xr_sem,
    ms_sem,
    mr_sem,
    es_sem,
    er_sem,
    vs_sem,
    vr_sem,
    bs_sem,
    br_sem,
    rs_sem,
    rr_sem,
    ts_sem,
    tr_sem,
    gs_sem,
    gr_sem,
):
    me = lax.axis_index("lists")
    rep = lax.axis_index("rep")
    core = lax.rem(me, 2)
    chip = me // 2
    sibling = me + 1 - 2 * core

    def copy_to(src, dst, ssem, rsem, **device):
        return pltpu.make_async_remote_copy(
            src, dst, ssem, rsem, device_id=device, device_id_type=MESH
        )

    pq_copy = pltpu.make_async_copy(pq_hbm, pq, pq_sem)
    pq_copy.start()
    cent_copy = pltpu.make_async_copy(
        cent_hbm.at[:, pl.ds(pl.multiple_of(rep * COLS, COLS), COLS)], cent, cent_sem
    )
    cent_copy.start()

    barrier = pltpu.get_barrier_semaphore()
    for k in range(1, N_REP):
        pl.semaphore_signal(
            barrier, inc=1, device_id={"rep": lax.rem(rep + k, N_REP)}, device_id_type=MESH
        )

    def greet(peer):
        pl.semaphore_signal(barrier, inc=1, device_id={"lists": peer}, device_id_type=MESH)

    each_peer(me, greet)

    scale = scale_ref[...].astype(F32)
    new = new_ref[...]
    owner = new // LISTS
    new_in = new - owner * LISTS + 1
    old_in = old_ref[...] - me * LISTS
    own_row = jnp.broadcast_to(owner.astype(F32), (ROWS, ROWS))
    own_col = jnp.transpose(own_row)
    earlier = (own_row == own_col) & (iota((ROWS, ROWS), 0) < iota((ROWS, ROWS), 1))
    rank = jnp.sum(jnp.where(earlier, 1.0, 0.0), axis=0, keepdims=True)
    target = owner.astype(F32) * 2.0 + rank
    new_hi = new_in // 256
    old_hi = old_in // 256
    shape = (N_REP * 32, 64)
    line = iota(shape, 0)
    pick = (line // 32) * 16 + 2 * lax.rem(line, 16) + lax.rem(line, 32) // 16
    pick = jnp.where(lax.rem(line, 16) < 8, pick, -1)
    chooser = jnp.where(pick == iota(shape, 1), 1.0, 0.0).astype(BF16)
    pq_copy.wait()
    meta = dot(chooser, pq[...].astype(F32).astype(BF16))
    line = lax.rem(iota((N_REP * 32, ROWS), 0), 32)
    extra = (
        (8, (new_in - new_hi * 256).astype(F32)),
        (24, new_hi.astype(F32)),
        (9, scale),
        (10, target),
        (11, (old_in - old_hi * 256).astype(F32)),
        (27, old_hi.astype(F32)),
    )
    for at, row in extra:
        meta = jnp.where(line == at, row, meta)
    msend[...] = meta.astype(BF16).reshape(N_REP, 32, ROWS)

    pl.semaphore_wait(barrier, N_LISTS - 1 + N_REP - 1)

    for k in range(1, N_REP):
        peer = lax.rem(rep + k, N_REP)
        copy_to(msend.at[peer], mrecv.at[rep], ms_sem, mr_sem, rep=peer).start()
    for k in range(1, N_REP):
        peer = lax.rem(rep + k, N_REP)
        copy_to(
            codes_hbm.at[:, pl.ds(pl.multiple_of(peer * COLS, COLS), COLS)],
            xbuf.at[rep],
            xs_sem,
            xr_sem,
            rep=peer,
        ).start()
    own = pltpu.make_async_copy(
        codes_hbm.at[:, pl.ds(pl.multiple_of(rep * COLS, COLS), COLS)], xbuf.at[rep], loc_sem
    )
    own.start()
    mrecv[rep] = msend[rep]
    peer = lax.rem(rep + 1, N_REP)
    three = mrecv.at[pl.ds(0, N_REP - 1)]
    wait = copy_to(three, three, ms_sem, mr_sem, rep=peer)
    wait.wait_recv()
    wait.wait_send()

    low = jnp.concatenate([mrecv[s, 0:16, :] for s in range(N_REP)], axis=1).astype(F32)
    high = jnp.concatenate([mrecv[s, 16:32, :] for s in range(N_REP)], axis=1).astype(F32)
    target = low[10:11, :].astype(I32)
    owner = target // 2
    slot = (iota((1, GROUP), 1) // ROWS) * 2 + target - owner * 2
    at_owner = jnp.where(iota((N_LISTS, GROUP), 0) == owner, 1.0, 0.0).astype(BF16)
    slot_b = jnp.broadcast_to(slot, (KK, GROUP))
    low_s = jnp.concatenate([jnp.where(slot_b == q, low, 0.0) for q in range(SLOTS)], axis=0)
    high_s = jnp.concatenate([jnp.where(slot_b == q, high, 0.0) for q in range(SLOTS)], axis=0)
    routed = dot(at_owner, low_s.astype(BF16), NT) + 256.0 * dot(
        at_owner, high_s.astype(BF16), NT
    )
    esend[...] = routed.reshape(N_LISTS, 1, SLOTS * KK)

    def send_meta(peer):
        copy_to(esend.at[peer], erecv.at[me], es_sem, er_sem, lists=peer).start()

    each_peer(me, send_meta)
    erecv[me] = esend[me]

    own.wait()
    three = xbuf.at[pl.ds(0, N_REP - 1)]
    wait = copy_to(three, three, xs_sem, xr_sem, rep=peer)
    wait.wait_recv()
    wait.wait_send()
    place = owner * SLOTS + slot
    x = xbuf[...].reshape(GROUP, COLS)
    move = jnp.where(iota((N_LISTS * SLOTS, GROUP), 0) == place, 1.0, 0.0).astype(BF16)
    moved = dot(move, x).reshape(N_LISTS, SLOTS, COLS)
    vsend[...] = jnp.concatenate([moved[:, :, 0:128], moved[:, :, 128:256]], axis=1).astype(BF16)

    def send_vec(peer):
        copy_to(vsend.at[peer], vrecv.at[me], vs_sem, vr_sem, lists=peer).start()

    each_peer(me, send_vec)
    vrecv[me] = vsend[me]

    scale = low[9:10, :]
    old_in = low[11:12, :] + 256.0 * high[11:12, :]
    weight = jnp.where(iota((LISTS, GROUP), 0).astype(F32) == old_in, scale, 0.0).astype(BF16)
    delta_acc[...] = dot(weight, x)
    pqk[0:8, 0:GROUP] = low[0:8, :]
    pqk[8:16, 0:GROUP] = high[0:8, :]
    lane_sub = iota((KSUB, 128), 1) // 16
    code = iota((KSUB, GROUP), 0).astype(F32).astype(BF16)
    scale_b = jnp.broadcast_to(scale.astype(BF16), (KSUB, GROUP))
    none = jnp.zeros((), BF16)
    for half in range(2):
        cols = x[:, half * 128 : (half + 1) * 128]

        def value_sums(i, total):
            row = (i // 4) * 8 + half * 4 + lax.rem(i, 4)
            picks = pqk[pl.ds(row, 1), 0:GROUP].astype(BF16)
            hits = jnp.where(code == picks, scale_b, none)
            sub = 2 * lax.rem(i, 4) + i // 4
            return jnp.where(lane_sub == sub, dot(hits, cols), total)

        book[half * KSUB : (half + 1) * KSUB, :] = lax.fori_loop(
            0, 8, value_sums, jnp.zeros((KSUB, 128), F32), unroll=UNROLL
        )

    cent_copy.wait()
    eye = jnp.where(iota((COLS, COLS), 0) == iota((COLS, COLS), 1), 1.0, 0.0).astype(BF16)
    cent_t = dot(eye, cent[...], NT).astype(BF16)

    most = erecv.at[pl.ds(0, N_LISTS - 1)]
    wait = copy_to(most, most, es_sem, er_sem, lists=sibling)
    wait.wait_recv()
    wait.wait_send()
    got = jnp.transpose(erecv[...].reshape(N_LISTS, SLOTS * KK))
    new_rows = []
    scale_rows = []
    for q in range(SLOTS):
        pairs = got[q * KK : q * KK + 8, :]
        odd = jnp.floor(pairs * (1.0 / 256.0))
        pqk[0:8, q * 128 : (q + 1) * 128] = pairs - 256.0 * odd
        pqk[8:16, q * 128 : (q + 1) * 128] = odd
        new_rows.append(got[q * KK + 8 : q * KK + 9, :])
        scale_rows.append(got[q * KK + 9 : q * KK + 10, :])
    new_in = jnp.concatenate(new_rows, axis=1) - 1.0
    new_scale = jnp.concatenate(scale_rows, axis=1)
    inside = iota((LISTS, N_LISTS * SLOTS), 0).astype(F32) == new_in
    centg[...] = dot(cent_t, jnp.where(inside, 1.0, 0.0).astype(BF16)).astype(BF16)
    code = iota((KSUB, N_LISTS * SLOTS), 0).astype(F32).astype(BF16)
    one = jnp.ones((), BF16)
    pairs = []
    for half in range(2):
        cols = centg[half * 128 : (half + 1) * 128, :]

        def cent_sums(i, total):
            row = (i // 4) * 8 + half * 4 + lax.rem(i, 4)
            picks = pqk[pl.ds(row, 1), :].astype(BF16)
            hits = jnp.where(code == picks, one, none)
            sub = 2 * lax.rem(i, 4) + i // 4
            return jnp.where(lane_sub == sub, dot(hits, cols, NT), total)

        total = lax.fori_loop(0, 8, cent_sums, jnp.zeros((KSUB, 128), F32), unroll=UNROLL)
        part = pl.ds(half * 16, 16)
        comb[part] = (book[half * KSUB : (half + 1) * KSUB, :] - total).reshape(16, 2, 8, 128)
        pair = copy_to(
            comb.at[part, 1 - core], sib.at[part], bs_sem.at[half], br_sem.at[half], lists=sibling
        )
        pair.start()
        pairs.append(pair)

    def send_tile(q, carry):
        there = 2 * q + core

        @pl.when(there != chip)
        def _():
            copy_to(
                sib.at[q], rsbuf.at[chip], rs_sem, rr_sem, lists=2 * there + core
            ).start()

        return carry

    for half in range(2):
        part = pl.ds(half * 16, 16)
        pairs[half].wait()
        sib[part] = sib[part] + comb[part, core]
        lax.fori_loop(half * 16, half * 16 + 16, send_tile, 0)
    sums_here = lax.rem(chip, 2) == core

    @pl.when(sums_here)
    def _():
        rsbuf[chip] = sib[chip // 2]
        most = rsbuf.at[pl.ds(0, CHIPS - 1)]
        copy_to(most, most, rs_sem, rr_sem, lists=sibling).wait_recv()
        total = jnp.sum(rsbuf[...], axis=0)
        shift = lax.rem(iota((8, 128), 1) // 16 - iota((8, 128), 0) + 8, 8)
        turned = total
        for d in range(1, 8):
            moved = pltpu.roll(pltpu.roll(total, 8 - d, 0), 16 * d, 1)
            turned = jnp.where(shift == d, moved, turned)
        tile[...] = turned
        gathered[core, chip // 2] = turned

        def send_sum(there):
            copy_to(
                tile, gathered.at[core, chip // 2], gs_sem, gr_sem, lists=2 * there + core
            ).start()

        each_chip(chip, send_sum)

    most = vrecv.at[pl.ds(0, N_LISTS - 1)]
    wait = copy_to(most, most, vs_sem, vr_sem, lists=sibling)
    wait.wait_recv()
    wait.wait_send()
    vflat[...] = vrecv[...].astype(F32).reshape(N_LISTS * 16, 128)
    vecs = jnp.concatenate(
        [
            jnp.concatenate(
                [vflat[pl.ds(h * 8 + q, N_LISTS, stride=16), :].astype(BF16) for h in range(2)],
                axis=1,
            )
            for q in range(SLOTS)
        ],
        axis=0,
    )
    weight = jnp.where(inside, new_scale, 0.0).astype(BF16)
    delta_out[...] = (dot(weight, vecs) - delta_acc[...]).astype(BF16)

    @pl.when(sums_here)
    def _():
        most = gathered.at[core, pl.ds(0, CHIPS // 2 - 1)]
        copy_to(most, most, gs_sem, gr_sem, lists=sibling).wait_recv()

    @pl.when(jnp.logical_not(sums_here))
    def _():
        most = gathered.at[core]
        copy_to(most, most, gs_sem, gr_sem, lists=sibling).wait_recv()

    give = copy_to(gathered.at[core], gathered.at[core], ts_sem, tr_sem, lists=sibling)
    give.start()

    @pl.when(sums_here)
    def _():
        most = rsbuf.at[pl.ds(0, CHIPS - 1)]
        copy_to(most, most, gs_sem, gr_sem, lists=sibling).wait_send()
        most = sib.at[pl.ds(0, CHIPS // 2 - 1)]
        copy_to(most, most, rs_sem, rr_sem, lists=sibling).wait_send()

    @pl.when(jnp.logical_not(sums_here))
    def _():
        copy_to(sib, sib, rs_sem, rr_sem, lists=sibling).wait_send()

    give.wait()
    for t in range(CHIPS):
        half, block = t // 32, t % 32
        book_out[half * 8 : half * 8 + 8, block * 128 : (block + 1) * 128] = gathered[
            t % 2, t // 2
        ]


def body(vector_codes, row_scales, old_list, new_list, pq_codes, centroids):
    vmem = pl.BlockSpec(memory_space=pltpu.VMEM)
    hbm = pl.BlockSpec(memory_space=pltpu.HBM)
    return pl.pallas_call(
        kernel,
        name="rebuild_window",
        out_shape=(
            jax.ShapeDtypeStruct((LISTS, COLS), BF16),
            jax.ShapeDtypeStruct((16, 4096), F32),
        ),
        in_specs=[hbm] + [vmem] * 3 + [hbm] * 2,
        out_specs=(vmem, vmem),
        scratch_shapes=[
            pltpu.VMEM((64, ROWS), I32),
            pltpu.VMEM((LISTS, COLS), BF16),
            pltpu.VMEM((N_REP, ROWS, COLS), BF16),
            pltpu.VMEM((N_REP, 32, ROWS), BF16),
            pltpu.VMEM((N_REP, 32, ROWS), BF16),
            pltpu.VMEM((N_LISTS, 1, 128), F32),
            pltpu.VMEM((N_LISTS, 1, 128), F32),
            pltpu.VMEM((N_LISTS, 16, 128), BF16),
            pltpu.VMEM((N_LISTS, 16, 128), BF16),
            pltpu.VMEM((LISTS, COLS), F32),
            pltpu.VMEM((N_LISTS * 16, 128), F32),
            pltpu.VMEM((16, N_LISTS * SLOTS), F32),
            pltpu.VMEM((COLS, N_LISTS * SLOTS), BF16),
            pltpu.VMEM((2 * KSUB, 128), F32),
            pltpu.VMEM((CHIPS // 2, 8, 128), F32),
            pltpu.VMEM((CHIPS // 2, 2, 8, 128), F32),
            pltpu.VMEM((CHIPS, 8, 128), F32),
            pltpu.VMEM((8, 128), F32),
            pltpu.VMEM((2, CHIPS // 2, 8, 128), F32),
        ]
        + [pltpu.SemaphoreType.DMA] * 11
        + [pltpu.SemaphoreType.DMA((2,))] * 2
        + [pltpu.SemaphoreType.DMA] * 6,
        compiler_params=pltpu.CompilerParams(
            collective_id=0, has_side_effects=True, vmem_limit_bytes=56 * 1024 * 1024
        ),
    )(
        vector_codes,
        row_scales.reshape(1, ROWS),
        old_list.reshape(1, ROWS),
        new_list.reshape(1, ROWS),
        pq_codes.T,
        centroids,
    )


def solution(mesh):
    return jax.shard_map(
        body,
        mesh=mesh,
        in_specs=(
            P(("lists", "rep"), None),
            P(("lists", "rep")),
            P(("lists", "rep")),
            P(("lists", "rep")),
            P(("lists", "rep"), None),
            P("lists", None),
        ),
        out_specs=(P("lists", "rep"), P("rep", None)),
        check_vma=False,
    )
```

```python
import functools

import jax
import jax.numpy as jnp
from jax import lax
from jax.experimental import pallas as pl
from jax.experimental.pallas import tpu as pltpu
from jax.sharding import PartitionSpec as P

MESH = pl.DeviceIdType.MESH
F32 = jnp.float32
BF16 = jnp.bfloat16
I32 = jnp.int32

N_LISTS = 128
N_REP = 4
CHIPS = N_LISTS // 2
ROWS = 128
GROUP = ROWS * N_REP
LISTS = 512
COLS = 256
SLOTS = 8
KK = 16
KSUB = 256
STACK = 4
V1, V2, V3 = 4, 6, 8
NT = (((1,), (1,)), ((), ()))
NN = (((1,), (0,)), ((), ()))


def dot(a, b, dims=NN):
    return lax.dot_general(a, b, dims, preferred_element_type=F32)


def iota(shape, axis):
    return lax.broadcasted_iota(I32, shape, axis)


def wrap(value, size):
    return jnp.where(value >= size, value - size, value)


def each_peer(me, visit, first=0, last=8):
    y, z, core = me // 16 * 16, lax.rem(me // 2, 8), lax.rem(me, 2)
    places = [2 * wrap(z + i // 2, 8) + wrap(core + i % 2, 2) for i in range(16)]

    def step(t, carry):
        start = wrap(y + 16 * t, N_LISTS)
        for i in range(16):
            peer = wrap(start + 16 * (3 * (i // 2) % 8), N_LISTS) + places[i]
            if i == 0:

                @pl.when(t > 0)
                def _():
                    visit(peer)
            else:
                visit(peer)
        return carry

    lax.fori_loop(first, last, step, 0)


def each_chip(chip, visit):
    y, z = chip // 8 * 8, lax.rem(chip, 8)
    places = [wrap(z + i, 8) for i in range(8)]

    def step(t, carry):
        start = wrap(y + 8 * t, CHIPS)
        for i in range(8):
            there = wrap(start + 8 * (3 * i % 8), CHIPS) + places[i]
            if i == 0:

                @pl.when(t > 0)
                def _():
                    visit(there)
            else:
                visit(there)
        return carry

    lax.fori_loop(0, 8, step, 0)


def kernel(
    codes_hbm,
    scale_hbm,
    old_hbm,
    new_hbm,
    pq_hbm,
    cent_hbm,
    delta_out,
    book_out,
    scale_ref,
    old_ref,
    new_ref,
    pq,
    cent,
    xbuf,
    msend,
    mrecv,
    esend,
    erecv,
    vsend,
    vrecv,
    delta_acc,
    vflat,
    pqk,
    centg,
    book,
    sib,
    comb,
    rsbuf,
    tile,
    gathered,
    in_sem,
    pq_sem,
    cent_sem,
    loc_sem,
    xs_sem,
    xr_sem,
    ms_sem,
    mr_sem,
    es_sem,
    er_sem,
    vs_sem,
    vr_sem,
    bs_sem,
    br_sem,
    rs_sem,
    rr_sem,
    ts_sem,
    tr_sem,
    gs_sem,
    gr_sem,
    row_sem,
):
    me = lax.axis_index("lists")
    rep = lax.axis_index("rep")
    core = lax.rem(me, 2)
    chip = me // 2
    sibling = me + 1 - 2 * core

    def copy_to(src, dst, ssem, rsem, **device):
        return pltpu.make_async_remote_copy(
            src, dst, ssem, rsem, device_id=device, device_id_type=MESH
        )

    small_copies = [
        pltpu.make_async_copy(src, dst, in_sem.at[i])
        for i, (src, dst) in enumerate(
            ((new_hbm, new_ref), (old_hbm, old_ref), (scale_hbm, scale_ref))
        )
    ]
    for small in small_copies:
        small.start()
    pq_copy = pltpu.make_async_copy(pq_hbm, pq, pq_sem)
    pq_copy.start()
    cent_copy = pltpu.make_async_copy(
        cent_hbm.at[:, pl.ds(pl.multiple_of(rep * COLS, COLS), COLS)], cent, cent_sem
    )
    cent_copy.start()

    barrier = pltpu.get_barrier_semaphore()
    for k in range(1, N_REP):
        pl.semaphore_signal(
            barrier, inc=1, device_id={"rep": lax.rem(rep + k, N_REP)}, device_id_type=MESH
        )

    for k in range(1, 16):
        row_peer = me // 16 * 16 + lax.rem(me + k, 16)
        pl.semaphore_signal(barrier, inc=1, device_id={"lists": row_peer}, device_id_type=MESH)
    for k in range(1, 8):
        column_peer = lax.rem(me + 16 * k, N_LISTS)
        pl.semaphore_signal(barrier, inc=1, device_id={"lists": column_peer}, device_id_type=MESH)

    for small in small_copies:
        small.wait()
    scale = scale_ref[...].astype(F32)
    new = new_ref[...]
    owner = new // LISTS
    new_in = new - owner * LISTS + 1
    old_in = old_ref[...] - me * LISTS
    own_row = jnp.broadcast_to(owner.astype(F32), (ROWS, ROWS))
    own_col = jnp.transpose(own_row)
    earlier = (own_row == own_col) & (iota((ROWS, ROWS), 0) < iota((ROWS, ROWS), 1))
    rank = jnp.sum(jnp.where(earlier, 1.0, 0.0), axis=0, keepdims=True)
    target = owner.astype(F32) * 2.0 + rank
    new_hi = new_in // 256
    old_hi = old_in // 256
    shape = (N_REP * 32, 64)
    line = iota(shape, 0)
    pick = (line // 32) * 16 + 2 * lax.rem(line, 16) + lax.rem(line, 32) // 16
    pick = jnp.where(lax.rem(line, 16) < 8, pick, -1)
    chooser = jnp.where(pick == iota(shape, 1), 1.0, 0.0).astype(BF16)
    pq_copy.wait()
    meta = dot(chooser, pq[...].astype(F32).astype(BF16))
    line = lax.rem(iota((N_REP * 32, ROWS), 0), 32)
    extra = (
        (8, (new_in - new_hi * 256).astype(F32)),
        (24, new_hi.astype(F32)),
        (9, scale),
        (10, target),
        (11, (old_in - old_hi * 256).astype(F32)),
        (27, old_hi.astype(F32)),
    )
    for at, row in extra:
        meta = jnp.where(line == at, row, meta)
    msend[...] = meta.astype(BF16).reshape(N_REP, 32, ROWS)

    pl.semaphore_wait(barrier, N_REP - 1 + 15 + 7)
    for k in range(1, 8):
        column_peer = lax.rem(me + 16 * k, N_LISTS)
        pl.semaphore_signal(row_sem, inc=1, device_id={"lists": column_peer}, device_id_type=MESH)

    for k in range(1, N_REP):
        peer = lax.rem(rep + k, N_REP)
        copy_to(msend.at[peer], mrecv.at[rep], ms_sem, mr_sem, rep=peer).start()
    for k in range(1, N_REP):
        peer = lax.rem(rep + k, N_REP)
        copy_to(
            codes_hbm.at[:, pl.ds(pl.multiple_of(peer * COLS, COLS), COLS)],
            xbuf.at[rep],
            xs_sem,
            xr_sem,
            rep=peer,
        ).start()
    own = pltpu.make_async_copy(
        codes_hbm.at[:, pl.ds(pl.multiple_of(rep * COLS, COLS), COLS)], xbuf.at[rep], loc_sem
    )
    own.start()
    mrecv[rep] = msend[rep]
    peer = lax.rem(rep + 1, N_REP)
    three = mrecv.at[pl.ds(0, N_REP - 1)]
    wait = copy_to(three, three, ms_sem, mr_sem, rep=peer)
    wait.wait_recv()
    wait.wait_send()

    low = jnp.concatenate([mrecv[s, 0:16, :] for s in range(N_REP)], axis=1).astype(F32)
    high = jnp.concatenate([mrecv[s, 16:32, :] for s in range(N_REP)], axis=1).astype(F32)
    target = low[10:11, :].astype(I32)
    owner = target // 2
    slot = (iota((1, GROUP), 1) // ROWS) * 2 + target - owner * 2
    at_owner = jnp.where(iota((N_LISTS, GROUP), 0) == owner, 1.0, 0.0).astype(BF16)
    slot_b = jnp.broadcast_to(slot, (KK, GROUP))
    low_s = jnp.concatenate([jnp.where(slot_b == q, low, 0.0) for q in range(SLOTS)], axis=0)
    high_s = jnp.concatenate([jnp.where(slot_b == q, high, 0.0) for q in range(SLOTS)], axis=0)
    routed = dot(at_owner, low_s.astype(BF16), NT) + 256.0 * dot(
        at_owner, high_s.astype(BF16), NT
    )
    esend[...] = routed.reshape(N_LISTS, 1, SLOTS * KK)

    def send_meta(peer):
        copy_to(esend.at[peer], erecv.at[me], es_sem, er_sem, lists=peer).start()

    pl.semaphore_wait(row_sem, 7)
    each_peer(me, send_meta)
    erecv[me] = esend[me]

    own.wait()
    three = xbuf.at[pl.ds(0, N_REP - 1)]
    wait = copy_to(three, three, xs_sem, xr_sem, rep=peer)
    wait.wait_recv()
    wait.wait_send()
    place = owner * SLOTS + slot
    x = xbuf[...].reshape(GROUP, COLS)
    move = jnp.where(iota((N_LISTS * SLOTS, GROUP), 0) == place, 1.0, 0.0).astype(BF16)
    moved = dot(move, x).reshape(N_LISTS, SLOTS, COLS)
    vsend[...] = jnp.concatenate([moved[:, :, 0:128], moved[:, :, 128:256]], axis=1).astype(BF16)

    def send_vec(peer):
        copy_to(vsend.at[peer], vrecv.at[me], vs_sem, vr_sem, lists=peer).start()

    each_peer(me, send_vec, 0, V1)
    vrecv[me] = vsend[me]

    scale = low[9:10, :]
    old_in = low[11:12, :] + 256.0 * high[11:12, :]
    weight = jnp.where(iota((LISTS, GROUP), 0).astype(F32) == old_in, scale, 0.0).astype(BF16)
    delta_acc[...] = dot(weight, x)
    pqk[0:8, 0:GROUP] = low[0:8, :]
    pqk[8:16, 0:GROUP] = high[0:8, :]
    lane_sub = iota((KSUB, 128), 1) // 16
    code = iota((KSUB, GROUP), 0).astype(F32).astype(BF16)
    scale_b = jnp.broadcast_to(scale.astype(BF16), (KSUB, GROUP))
    none = jnp.zeros((), BF16)

    def code_sums(hits_of, half, cols, dims):
        total = jnp.zeros((KSUB, 128), F32)
        for first in range(0, 8, STACK):
            these = range(first, first + STACK)
            hits = [hits_of((i // 4) * 8 + half * 4 + i % 4) for i in these]
            sums = dot(jnp.concatenate(hits, axis=0), cols, dims)
            for at, i in enumerate(these):
                own = lane_sub == 2 * (i % 4) + i // 4
                total = jnp.where(own, sums[at * KSUB : (at + 1) * KSUB, :], total)
        return total

    for half in range(2):
        cols = x[:, half * 128 : (half + 1) * 128]

        def value_hits(row):
            return jnp.where(code == pqk[row : row + 1, 0:GROUP].astype(BF16), scale_b, none)

        book[half * KSUB : (half + 1) * KSUB, :] = code_sums(value_hits, half, cols, NN)

    cent_copy.wait()
    eye = jnp.where(iota((COLS, COLS), 0) == iota((COLS, COLS), 1), 1.0, 0.0).astype(BF16)
    cent_t = dot(eye, cent[...], NT).astype(BF16)

    most = erecv.at[pl.ds(0, N_LISTS - 1)]
    wait = copy_to(most, most, es_sem, er_sem, lists=sibling)
    wait.wait_recv()
    wait.wait_send()
    each_peer(me, send_vec, V1, V2)
    got = jnp.transpose(erecv[...].reshape(N_LISTS, SLOTS * KK))
    new_rows = []
    scale_rows = []
    for q in range(SLOTS):
        pairs = got[q * KK : q * KK + 8, :]
        odd = jnp.floor(pairs * (1.0 / 256.0))
        pqk[0:8, q * 128 : (q + 1) * 128] = pairs - 256.0 * odd
        pqk[8:16, q * 128 : (q + 1) * 128] = odd
        new_rows.append(got[q * KK + 8 : q * KK + 9, :])
        scale_rows.append(got[q * KK + 9 : q * KK + 10, :])
    new_in = jnp.concatenate(new_rows, axis=1) - 1.0
    new_scale = jnp.concatenate(scale_rows, axis=1)
    inside = iota((LISTS, N_LISTS * SLOTS), 0).astype(F32) == new_in
    centg[...] = dot(cent_t, jnp.where(inside, 1.0, 0.0).astype(BF16)).astype(BF16)
    code = iota((KSUB, N_LISTS * SLOTS), 0).astype(F32).astype(BF16)
    one = jnp.ones((), BF16)
    pairs = []
    for half in range(2):
        cols = centg[half * 128 : (half + 1) * 128, :]

        def cent_hits(row):
            return jnp.where(code == pqk[row : row + 1, :].astype(BF16), one, none)

        total = code_sums(cent_hits, half, cols, NT)
        part = pl.ds(half * 16, 16)
        comb[part] = (book[half * KSUB : (half + 1) * KSUB, :] - total).reshape(16, 2, 8, 128)
        pair = copy_to(
            comb.at[part, 1 - core], sib.at[part], bs_sem.at[half], br_sem.at[half], lists=sibling
        )
        pair.start()
        pairs.append(pair)

    y, z = chip // 8, lax.rem(chip, 8)
    block = z // 4

    def send_tiles(half):
        def step(t, carry):
            row = wrap(y + t, 8)
            odd = lax.rem(row + half, 2)
            for i in range(2):
                col = wrap(block + i, 2)
                there = row * 8 + 4 * col + 2 * odd + core

                @pl.when(there != chip)
                def _():
                    copy_to(
                        sib.at[half * 16 + row * 2 + col],
                        rsbuf.at[chip],
                        rs_sem,
                        rr_sem,
                        lists=2 * there + core,
                    ).start()

            return carry

        lax.fori_loop(0, 8, step, 0)

    for half in range(2):
        part = pl.ds(half * 16, 16)
        pairs[half].wait()
        sib[part] = sib[part] + comb[part, core]
        send_tiles(half)
    each_peer(me, send_vec, V2, V3)
    mine = lax.rem(y + z // 2, 2) * 16 + y * 2 + block
    sums_here = lax.rem(z, 2) == core

    @pl.when(sums_here)
    def _():
        rsbuf[chip] = sib[mine]
        most = rsbuf.at[pl.ds(0, CHIPS - 1)]
        copy_to(most, most, rs_sem, rr_sem, lists=sibling).wait_recv()
        total = jnp.sum(rsbuf[...], axis=0)
        shift = lax.rem(iota((8, 128), 1) // 16 - iota((8, 128), 0) + 8, 8)
        turned = total
        for d in range(1, 8):
            moved = pltpu.roll(pltpu.roll(total, 8 - d, 0), 16 * d, 1)
            turned = jnp.where(shift == d, moved, turned)
        tile[...] = turned
        gathered[core, mine] = turned

        def send_sum(there):
            copy_to(
                tile, gathered.at[core, mine], gs_sem, gr_sem, lists=2 * there + core
            ).start()

        each_chip(chip, send_sum)

    each_peer(me, send_vec, V3, 8)

    most = vrecv.at[pl.ds(0, N_LISTS - 1)]
    wait = copy_to(most, most, vs_sem, vr_sem, lists=sibling)
    wait.wait_recv()
    wait.wait_send()
    vflat[...] = vrecv[...].astype(F32).reshape(N_LISTS * 16, 128)
    vecs = jnp.concatenate(
        [
            jnp.concatenate(
                [vflat[pl.ds(h * 8 + q, N_LISTS, stride=16), :].astype(BF16) for h in range(2)],
                axis=1,
            )
            for q in range(SLOTS)
        ],
        axis=0,
    )
    weight = jnp.where(inside, new_scale, 0.0).astype(BF16)
    delta_out[...] = (dot(weight, vecs) - delta_acc[...]).astype(BF16)

    @pl.when(sums_here)
    def _():
        most = gathered.at[core, pl.ds(0, CHIPS // 2 - 1)]
        copy_to(most, most, gs_sem, gr_sem, lists=sibling).wait_recv()

    @pl.when(jnp.logical_not(sums_here))
    def _():
        most = gathered.at[core]
        copy_to(most, most, gs_sem, gr_sem, lists=sibling).wait_recv()

    give = copy_to(gathered.at[core], gathered.at[core], ts_sem, tr_sem, lists=sibling)
    give.start()

    @pl.when(sums_here)
    def _():
        most = rsbuf.at[pl.ds(0, CHIPS - 1)]
        copy_to(most, most, gs_sem, gr_sem, lists=sibling).wait_send()
        most = sib.at[pl.ds(0, CHIPS // 2 - 1)]
        copy_to(most, most, rs_sem, rr_sem, lists=sibling).wait_send()

    @pl.when(jnp.logical_not(sums_here))
    def _():
        copy_to(sib, sib, rs_sem, rr_sem, lists=sibling).wait_send()

    give.wait()
    for t in range(CHIPS):
        half, block = t // 32, t % 32
        book_out[half * 8 : half * 8 + 8, block * 128 : (block + 1) * 128] = gathered[
            t % 2, t // 2
        ]


def body(vector_codes, row_scales, old_list, new_list, pq_codes, centroids):
    vmem = pl.BlockSpec(memory_space=pltpu.VMEM)
    hbm = pl.BlockSpec(memory_space=pltpu.HBM)
    return pl.pallas_call(
        kernel,
        name="rebuild_window",
        out_shape=(
            pltpu.VMEM((LISTS, COLS), BF16),
            pltpu.VMEM((16, 4096), F32),
        ),
        in_specs=[hbm] * 6,
        out_specs=(vmem, vmem),
        scratch_shapes=[
            pltpu.VMEM((1, ROWS), BF16),
            pltpu.VMEM((1, ROWS), I32),
            pltpu.VMEM((1, ROWS), I32),
            pltpu.VMEM((64, ROWS), I32),
            pltpu.VMEM((LISTS, COLS), BF16),
            pltpu.VMEM((N_REP, ROWS, COLS), BF16),
            pltpu.VMEM((N_REP, 32, ROWS), BF16),
            pltpu.VMEM((N_REP, 32, ROWS), BF16),
            pltpu.VMEM((N_LISTS, 1, 128), F32),
            pltpu.VMEM((N_LISTS, 1, 128), F32),
            pltpu.VMEM((N_LISTS, 16, 128), BF16),
            pltpu.VMEM((N_LISTS, 16, 128), BF16),
            pltpu.VMEM((LISTS, COLS), F32),
            pltpu.VMEM((N_LISTS * 16, 128), F32),
            pltpu.VMEM((16, N_LISTS * SLOTS), F32),
            pltpu.VMEM((COLS, N_LISTS * SLOTS), BF16),
            pltpu.VMEM((2 * KSUB, 128), F32),
            pltpu.VMEM((CHIPS // 2, 8, 128), F32),
            pltpu.VMEM((CHIPS // 2, 2, 8, 128), F32),
            pltpu.VMEM((CHIPS, 8, 128), F32),
            pltpu.VMEM((8, 128), F32),
            pltpu.VMEM((2, CHIPS // 2, 8, 128), F32),
        ]
        + [pltpu.SemaphoreType.DMA((3,))]
        + [pltpu.SemaphoreType.DMA] * 11
        + [pltpu.SemaphoreType.DMA((2,))] * 2
        + [pltpu.SemaphoreType.DMA] * 6
        + [pltpu.SemaphoreType.REGULAR],
        compiler_params=pltpu.CompilerParams(
            collective_id=0, has_side_effects=True, vmem_limit_bytes=56 * 1024 * 1024
        ),
    )(
        vector_codes,
        row_scales.reshape(1, ROWS),
        old_list.reshape(1, ROWS),
        new_list.reshape(1, ROWS),
        pq_codes.T,
        centroids,
    )


def solution(mesh):
    return jax.shard_map(
        body,
        mesh=mesh,
        in_specs=(
            P(("lists", "rep"), None),
            P(("lists", "rep")),
            P(("lists", "rep")),
            P(("lists", "rep")),
            P(("lists", "rep"), None),
            P("lists", None),
        ),
        out_specs=(P("lists", "rep"), P("rep", None)),
        check_vma=False,
    )
```

```python
import functools

import jax
import jax.numpy as jnp
from jax import lax
from jax.experimental import pallas as pl
from jax.experimental.pallas import tpu as pltpu
from jax.sharding import PartitionSpec as P

MESH = pl.DeviceIdType.MESH
F32 = jnp.float32
BF16 = jnp.bfloat16
I32 = jnp.int32

N_LISTS = 128
N_REP = 4
CHIPS = N_LISTS // 2
ROWS = 128
GROUP = ROWS * N_REP
LISTS = 512
COLS = 256
SLOTS = 8
KK = 16
KSUB = 256
STACK = 4
V1, V2, V3 = 4, 6, 8
NT = (((1,), (1,)), ((), ()))
NN = (((1,), (0,)), ((), ()))


def dot(a, b, dims=NN):
    return lax.dot_general(a, b, dims, preferred_element_type=F32)


def iota(shape, axis):
    return lax.broadcasted_iota(I32, shape, axis)


def wrap(value, size):
    return jnp.where(value >= size, value - size, value)


def each_peer(me, visit, first=0, last=8):
    y, z, core = me // 16 * 16, lax.rem(me // 2, 8), lax.rem(me, 2)
    places = [2 * wrap(z + i // 2, 8) + wrap(core + i % 2, 2) for i in range(16)]

    def step(t, carry):
        start = wrap(y + 16 * t, N_LISTS)
        for i in range(16):
            peer = wrap(start + 16 * (3 * (i // 2) % 8), N_LISTS) + places[i]
            if i == 0:

                @pl.when(t > 0)
                def _():
                    visit(peer)
            else:
                visit(peer)
        return carry

    lax.fori_loop(first, last, step, 0)


def hops(step):
    return min(step, 8 - step)


FAR_FIRST = sorted(
    ((dy, dz) for dy in range(8) for dz in range(8)), key=lambda d: -hops(d[0]) - hops(d[1])
)
FAR_RING = sorted(range(1, 8), key=lambda d: -hops(d))


def kernel(
    codes_hbm,
    scale_hbm,
    old_hbm,
    new_hbm,
    pq_hbm,
    cent_hbm,
    delta_out,
    book_out,
    scale_ref,
    old_ref,
    new_ref,
    pq,
    cent,
    xbuf,
    msend,
    mrecv,
    esend,
    erecv,
    vsend,
    vrecv,
    delta_acc,
    vflat,
    pqk,
    centg,
    book,
    sib,
    comb,
    rsbuf,
    tile,
    gathered,
    in_sem,
    pq_sem,
    cent_sem,
    loc_sem,
    xs_sem,
    xr_sem,
    ms_sem,
    mr_sem,
    es_sem,
    er_sem,
    vs_sem,
    vr_sem,
    bs_sem,
    br_sem,
    rs_sem,
    rr_sem,
    ts_sem,
    tr_sem,
    gs_sem,
    gr_sem,
    row_sem,
):
    me = lax.axis_index("lists")
    rep = lax.axis_index("rep")
    core = lax.rem(me, 2)
    chip = me // 2
    sibling = me + 1 - 2 * core

    def copy_to(src, dst, ssem, rsem, **device):
        return pltpu.make_async_remote_copy(
            src, dst, ssem, rsem, device_id=device, device_id_type=MESH
        )

    small_copies = [
        pltpu.make_async_copy(src, dst, in_sem.at[i])
        for i, (src, dst) in enumerate(
            ((new_hbm, new_ref), (old_hbm, old_ref), (scale_hbm, scale_ref))
        )
    ]
    for small in small_copies:
        small.start()
    pq_copy = pltpu.make_async_copy(pq_hbm, pq, pq_sem)
    pq_copy.start()
    cent_copy = pltpu.make_async_copy(
        cent_hbm.at[:, pl.ds(pl.multiple_of(rep * COLS, COLS), COLS)], cent, cent_sem
    )
    cent_copy.start()

    barrier = pltpu.get_barrier_semaphore()
    y, z = chip // 8, lax.rem(chip, 8)
    rows = [16 * wrap(y + d, 8) for d in range(8)]
    places = [2 * wrap(z + d, 8) for d in range(8)]
    for k in (2, 1, 3):
        pl.semaphore_signal(
            barrier, inc=1, device_id={"rep": lax.rem(rep + k, N_REP)}, device_id_type=MESH
        )

    for d in FAR_RING:
        for peer in (rows[d] + places[0] + core, rows[0] + places[d], rows[0] + places[d] + 1):
            pl.semaphore_signal(barrier, inc=1, device_id={"lists": peer}, device_id_type=MESH)
    pl.semaphore_signal(barrier, inc=1, device_id={"lists": sibling}, device_id_type=MESH)

    for small in small_copies:
        small.wait()
    scale = scale_ref[...].astype(F32)
    new = new_ref[...]
    owner = new // LISTS
    new_in = new - owner * LISTS + 1
    old_in = old_ref[...] - me * LISTS
    own_row = jnp.broadcast_to(owner.astype(F32), (ROWS, ROWS))
    own_col = jnp.transpose(own_row)
    earlier = (own_row == own_col) & (iota((ROWS, ROWS), 0) < iota((ROWS, ROWS), 1))
    rank = jnp.sum(jnp.where(earlier, 1.0, 0.0), axis=0, keepdims=True)
    target = owner.astype(F32) * 2.0 + rank
    new_hi = new_in // 256
    old_hi = old_in // 256
    shape = (N_REP * 32, 64)
    line = iota(shape, 0)
    pick = (line // 32) * 16 + 2 * lax.rem(line, 16) + lax.rem(line, 32) // 16
    pick = jnp.where(lax.rem(line, 16) < 8, pick, -1)
    chooser = jnp.where(pick == iota(shape, 1), 1.0, 0.0).astype(BF16)
    pq_copy.wait()
    meta = dot(chooser, pq[...].astype(F32).astype(BF16))
    line = lax.rem(iota((N_REP * 32, ROWS), 0), 32)
    extra = (
        (8, (new_in - new_hi * 256).astype(F32)),
        (24, new_hi.astype(F32)),
        (9, scale),
        (10, target),
        (11, (old_in - old_hi * 256).astype(F32)),
        (27, old_hi.astype(F32)),
    )
    for at, row in extra:
        meta = jnp.where(line == at, row, meta)
    msend[...] = meta.astype(BF16).reshape(N_REP, 32, ROWS)

    pl.semaphore_wait(barrier, N_REP - 1 + 15 + 7)
    for d in FAR_RING:
        column_peer = rows[d] + places[0] + core
        pl.semaphore_signal(row_sem, inc=1, device_id={"lists": column_peer}, device_id_type=MESH)

    for k in (2, 1, 3):
        peer = lax.rem(rep + k, N_REP)
        copy_to(msend.at[peer], mrecv.at[rep], ms_sem, mr_sem, rep=peer).start()
    for k in (2, 1, 3):
        peer = lax.rem(rep + k, N_REP)
        copy_to(
            codes_hbm.at[:, pl.ds(pl.multiple_of(peer * COLS, COLS), COLS)],
            xbuf.at[rep],
            xs_sem,
            xr_sem,
            rep=peer,
        ).start()
    own = pltpu.make_async_copy(
        codes_hbm.at[:, pl.ds(pl.multiple_of(rep * COLS, COLS), COLS)], xbuf.at[rep], loc_sem
    )
    own.start()
    mrecv[rep] = msend[rep]
    peer = lax.rem(rep + 1, N_REP)
    three = mrecv.at[pl.ds(0, N_REP - 1)]
    wait = copy_to(three, three, ms_sem, mr_sem, rep=peer)
    wait.wait_recv()
    wait.wait_send()

    low = jnp.concatenate([mrecv[s, 0:16, :] for s in range(N_REP)], axis=1).astype(F32)
    high = jnp.concatenate([mrecv[s, 16:32, :] for s in range(N_REP)], axis=1).astype(F32)
    target = low[10:11, :].astype(I32)
    owner = target // 2
    slot = (iota((1, GROUP), 1) // ROWS) * 2 + target - owner * 2
    at_owner = jnp.where(iota((N_LISTS, GROUP), 0) == owner, 1.0, 0.0).astype(BF16)
    slot_b = jnp.broadcast_to(slot, (KK, GROUP))
    low_s = jnp.concatenate([jnp.where(slot_b == q, low, 0.0) for q in range(SLOTS)], axis=0)
    high_s = jnp.concatenate([jnp.where(slot_b == q, high, 0.0) for q in range(SLOTS)], axis=0)
    routed = dot(at_owner, low_s.astype(BF16), NT) + 256.0 * dot(
        at_owner, high_s.astype(BF16), NT
    )
    esend[...] = routed.reshape(N_LISTS, 1, SLOTS * KK)

    def send_meta(peer):
        copy_to(esend.at[peer], erecv.at[me], es_sem, er_sem, lists=peer).start()

    pl.semaphore_wait(row_sem, 7)
    for dy, dz in FAR_FIRST[:-1]:
        send_meta(rows[dy] + places[dz])
        send_meta(rows[dy] + places[dz] + 1)
    send_meta(sibling)
    erecv[me] = esend[me]

    own.wait()
    three = xbuf.at[pl.ds(0, N_REP - 1)]
    wait = copy_to(three, three, xs_sem, xr_sem, rep=peer)
    wait.wait_recv()
    wait.wait_send()
    place = owner * SLOTS + slot
    x = xbuf[...].reshape(GROUP, COLS)
    move = jnp.where(iota((N_LISTS * SLOTS, GROUP), 0) == place, 1.0, 0.0).astype(BF16)
    moved = dot(move, x).reshape(N_LISTS, SLOTS, COLS)
    vsend[...] = jnp.concatenate([moved[:, :, 0:128], moved[:, :, 128:256]], axis=1).astype(BF16)

    def send_vec(peer):
        copy_to(vsend.at[peer], vrecv.at[me], vs_sem, vr_sem, lists=peer).start()

    each_peer(me, send_vec, 0, V1)
    vrecv[me] = vsend[me]

    scale = low[9:10, :]
    old_in = low[11:12, :] + 256.0 * high[11:12, :]
    weight = jnp.where(iota((LISTS, GROUP), 0).astype(F32) == old_in, scale, 0.0).astype(BF16)
    delta_acc[...] = dot(weight, x)
    pqk[0:8, 0:GROUP] = low[0:8, :]
    pqk[8:16, 0:GROUP] = high[0:8, :]
    lane_sub = iota((KSUB, 128), 1) // 16
    code = iota((KSUB, GROUP), 0).astype(F32).astype(BF16)
    scale_b = jnp.broadcast_to(scale.astype(BF16), (KSUB, GROUP))
    none = jnp.zeros((), BF16)

    def code_sums(hits_of, half, cols, dims):
        total = jnp.zeros((KSUB, 128), F32)
        for first in range(0, 8, STACK):
            these = range(first, first + STACK)
            hits = [hits_of((i // 4) * 8 + half * 4 + i % 4) for i in these]
            sums = dot(jnp.concatenate(hits, axis=0), cols, dims)
            for at, i in enumerate(these):
                own = lane_sub == 2 * (i % 4) + i // 4
                total = jnp.where(own, sums[at * KSUB : (at + 1) * KSUB, :], total)
        return total

    for half in range(2):
        cols = x[:, half * 128 : (half + 1) * 128]

        def value_hits(row):
            return jnp.where(code == pqk[row : row + 1, 0:GROUP].astype(BF16), scale_b, none)

        book[half * KSUB : (half + 1) * KSUB, :] = code_sums(value_hits, half, cols, NN)

    cent_copy.wait()
    eye = jnp.where(iota((COLS, COLS), 0) == iota((COLS, COLS), 1), 1.0, 0.0).astype(BF16)
    cent_t = dot(eye, cent[...], NT).astype(BF16)

    most = erecv.at[pl.ds(0, N_LISTS - 1)]
    wait = copy_to(most, most, es_sem, er_sem, lists=sibling)
    wait.wait_recv()
    wait.wait_send()
    each_peer(me, send_vec, V1, V2)
    got = jnp.transpose(erecv[...].reshape(N_LISTS, SLOTS * KK))
    new_rows = []
    scale_rows = []
    for q in range(SLOTS):
        pairs = got[q * KK : q * KK + 8, :]
        odd = jnp.floor(pairs * (1.0 / 256.0))
        pqk[0:8, q * 128 : (q + 1) * 128] = pairs - 256.0 * odd
        pqk[8:16, q * 128 : (q + 1) * 128] = odd
        new_rows.append(got[q * KK + 8 : q * KK + 9, :])
        scale_rows.append(got[q * KK + 9 : q * KK + 10, :])
    new_in = jnp.concatenate(new_rows, axis=1) - 1.0
    new_scale = jnp.concatenate(scale_rows, axis=1)
    inside = iota((LISTS, N_LISTS * SLOTS), 0).astype(F32) == new_in
    centg[...] = dot(cent_t, jnp.where(inside, 1.0, 0.0).astype(BF16)).astype(BF16)
    code = iota((KSUB, N_LISTS * SLOTS), 0).astype(F32).astype(BF16)
    one = jnp.ones((), BF16)
    pairs = []
    for half in range(2):
        cols = centg[half * 128 : (half + 1) * 128, :]

        def cent_hits(row):
            return jnp.where(code == pqk[row : row + 1, :].astype(BF16), one, none)

        total = code_sums(cent_hits, half, cols, NT)
        part = pl.ds(half * 16, 16)
        comb[part] = (book[half * KSUB : (half + 1) * KSUB, :] - total).reshape(16, 2, 8, 128)
        pair = copy_to(
            comb.at[part, 1 - core], sib.at[part], bs_sem.at[half], br_sem.at[half], lists=sibling
        )
        pair.start()
        pairs.append(pair)

    block = z // 4

    def send_tiles(half):
        def send_tile(dy, near):
            row = wrap(y + dy, 8)
            place = 2 * lax.rem(row + half, 2) + core
            ahead = wrap(place - z + 8, 8)
            close = (ahead <= 2) | (ahead >= 6)
            col = jnp.where(close, 1 - near, near)
            there = row * 8 + 4 * col + place

            @pl.when(there != chip)
            def _():
                copy_to(
                    sib.at[half * 16 + row * 2 + col],
                    rsbuf.at[chip],
                    rs_sem,
                    rr_sem,
                    lists=2 * there + core,
                ).start()

        far_first = [(dy, near) for dy in range(8) for near in range(2)]
        for dy, near in sorted(far_first, key=lambda d: 2 * d[1] - hops(d[0])):
            send_tile(dy, near)

    for half in range(2):
        part = pl.ds(half * 16, 16)
        pairs[half].wait()
        sib[part] = sib[part] + comb[part, core]
        send_tiles(half)
    each_peer(me, send_vec, V2, V3)
    mine = lax.rem(y + z // 2, 2) * 16 + y * 2 + block
    sums_here = lax.rem(z, 2) == core

    @pl.when(sums_here)
    def _():
        rsbuf[chip] = sib[mine]
        most = rsbuf.at[pl.ds(0, CHIPS - 1)]
        copy_to(most, most, rs_sem, rr_sem, lists=sibling).wait_recv()
        total = jnp.sum(rsbuf[...], axis=0)
        shift = lax.rem(iota((8, 128), 1) // 16 - iota((8, 128), 0) + 8, 8)
        turned = total
        for d in range(1, 8):
            moved = pltpu.roll(pltpu.roll(total, 8 - d, 0), 16 * d, 1)
            turned = jnp.where(shift == d, moved, turned)
        tile[...] = turned
        gathered[core, mine] = turned

        def send_sum(peer):
            copy_to(
                tile, gathered.at[core, mine], gs_sem, gr_sem, lists=peer
            ).start()

        for dy, dz in FAR_FIRST[:-1]:
            send_sum(rows[dy] + places[dz] + core)

    each_peer(me, send_vec, V3, 8)

    most = vrecv.at[pl.ds(0, N_LISTS - 1)]
    wait = copy_to(most, most, vs_sem, vr_sem, lists=sibling)
    wait.wait_recv()
    wait.wait_send()
    vflat[...] = vrecv[...].astype(F32).reshape(N_LISTS * 16, 128)
    vecs = jnp.concatenate(
        [
            jnp.concatenate(
                [vflat[pl.ds(h * 8 + q, N_LISTS, stride=16), :].astype(BF16) for h in range(2)],
                axis=1,
            )
            for q in range(SLOTS)
        ],
        axis=0,
    )
    weight = jnp.where(inside, new_scale, 0.0).astype(BF16)
    delta_out[...] = (dot(weight, vecs) - delta_acc[...]).astype(BF16)

    @pl.when(sums_here)
    def _():
        most = gathered.at[core, pl.ds(0, CHIPS // 2 - 1)]
        copy_to(most, most, gs_sem, gr_sem, lists=sibling).wait_recv()

    @pl.when(jnp.logical_not(sums_here))
    def _():
        most = gathered.at[core]
        copy_to(most, most, gs_sem, gr_sem, lists=sibling).wait_recv()

    give = copy_to(gathered.at[core], gathered.at[core], ts_sem, tr_sem, lists=sibling)
    give.start()

    @pl.when(sums_here)
    def _():
        most = rsbuf.at[pl.ds(0, CHIPS - 1)]
        copy_to(most, most, gs_sem, gr_sem, lists=sibling).wait_send()
        most = sib.at[pl.ds(0, CHIPS // 2 - 1)]
        copy_to(most, most, rs_sem, rr_sem, lists=sibling).wait_send()

    @pl.when(jnp.logical_not(sums_here))
    def _():
        copy_to(sib, sib, rs_sem, rr_sem, lists=sibling).wait_send()

    give.wait()
    for t in range(CHIPS):
        half, block = t // 32, t % 32
        book_out[half * 8 : half * 8 + 8, block * 128 : (block + 1) * 128] = gathered[
            t % 2, t // 2
        ]


def body(vector_codes, row_scales, old_list, new_list, pq_codes, centroids):
    vmem = pl.BlockSpec(memory_space=pltpu.VMEM)
    hbm = pl.BlockSpec(memory_space=pltpu.HBM)
    return pl.pallas_call(
        kernel,
        name="rebuild_window",
        out_shape=(
            pltpu.VMEM((LISTS, COLS), BF16),
            pltpu.VMEM((16, 4096), F32),
        ),
        in_specs=[hbm] * 6,
        out_specs=(vmem, vmem),
        scratch_shapes=[
            pltpu.VMEM((1, ROWS), BF16),
            pltpu.VMEM((1, ROWS), I32),
            pltpu.VMEM((1, ROWS), I32),
            pltpu.VMEM((64, ROWS), I32),
            pltpu.VMEM((LISTS, COLS), BF16),
            pltpu.VMEM((N_REP, ROWS, COLS), BF16),
            pltpu.VMEM((N_REP, 32, ROWS), BF16),
            pltpu.VMEM((N_REP, 32, ROWS), BF16),
            pltpu.VMEM((N_LISTS, 1, 128), F32),
            pltpu.VMEM((N_LISTS, 1, 128), F32),
            pltpu.VMEM((N_LISTS, 16, 128), BF16),
            pltpu.VMEM((N_LISTS, 16, 128), BF16),
            pltpu.VMEM((LISTS, COLS), F32),
            pltpu.VMEM((N_LISTS * 16, 128), F32),
            pltpu.VMEM((16, N_LISTS * SLOTS), F32),
            pltpu.VMEM((COLS, N_LISTS * SLOTS), BF16),
            pltpu.VMEM((2 * KSUB, 128), F32),
            pltpu.VMEM((CHIPS // 2, 8, 128), F32),
            pltpu.VMEM((CHIPS // 2, 2, 8, 128), F32),
            pltpu.VMEM((CHIPS, 8, 128), F32),
            pltpu.VMEM((8, 128), F32),
            pltpu.VMEM((2, CHIPS // 2, 8, 128), F32),
        ]
        + [pltpu.SemaphoreType.DMA((3,))]
        + [pltpu.SemaphoreType.DMA] * 11
        + [pltpu.SemaphoreType.DMA((2,))] * 2
        + [pltpu.SemaphoreType.DMA] * 6
        + [pltpu.SemaphoreType.REGULAR],
        compiler_params=pltpu.CompilerParams(
            collective_id=0, has_side_effects=True, vmem_limit_bytes=56 * 1024 * 1024
        ),
    )(
        vector_codes,
        row_scales.reshape(1, ROWS),
        old_list.reshape(1, ROWS),
        new_list.reshape(1, ROWS),
        pq_codes.T,
        centroids,
    )


def solution(mesh):
    return jax.shard_map(
        body,
        mesh=mesh,
        in_specs=(
            P(("lists", "rep"), None),
            P(("lists", "rep")),
            P(("lists", "rep")),
            P(("lists", "rep")),
            P(("lists", "rep"), None),
            P("lists", None),
        ),
        out_specs=(P("lists", "rep"), P("rep", None)),
        check_vma=False,
    )
```

```python
import functools

import jax
import jax.numpy as jnp
from jax import lax
from jax.experimental import pallas as pl
from jax.experimental.pallas import tpu as pltpu
from jax.sharding import PartitionSpec as P

MESH = pl.DeviceIdType.MESH
F32 = jnp.float32
BF16 = jnp.bfloat16
I32 = jnp.int32

N_LISTS = 128
N_REP = 4
CHIPS = N_LISTS // 2
ROWS = 128
GROUP = ROWS * N_REP
LISTS = 512
COLS = 256
SLOTS = 8
KK = 16
KSUB = 256
STACK = 4
V1, V2, V3 = 40, 40, 63
NT = (((1,), (1,)), ((), ()))
NN = (((1,), (0,)), ((), ()))


def dot(a, b, dims=NN):
    return lax.dot_general(a, b, dims, preferred_element_type=F32)


def iota(shape, axis):
    return lax.broadcasted_iota(I32, shape, axis)


def wrap(value, size):
    return jnp.where(value >= size, value - size, value)


def hops(step):
    return min(step, 8 - step)


NEAR_FIRST = sorted(
    ((dy, dz) for dy in range(8) for dz in range(8)), key=lambda d: hops(d[0]) + hops(d[1])
)
FAR_FIRST = NEAR_FIRST[:0:-1]
SPREAD = [(k * 27 % CHIPS // 8, k * 27 % 8) for k in range(1, CHIPS)]
HALF = N_LISTS // 2
FAR_RING = sorted(range(1, 8), key=lambda d: -hops(d))


def kernel(
    codes_hbm,
    scale_hbm,
    old_hbm,
    new_hbm,
    pq_hbm,
    cent_hbm,
    delta_out,
    book_out,
    scale_ref,
    old_ref,
    new_ref,
    pq,
    cent,
    xbuf,
    msend,
    mrecv,
    esend,
    erecv,
    vsend,
    vrecv,
    delta_acc,
    vflat,
    pqk,
    centg,
    book,
    sib,
    comb,
    rsbuf,
    tile,
    gathered,
    in_sem,
    pq_sem,
    cent_sem,
    loc_sem,
    xs_sem,
    xr_sem,
    ms_sem,
    mr_sem,
    es_sem,
    er_sem,
    vs_sem,
    vr_sem,
    bs_sem,
    br_sem,
    rs_sem,
    rr_sem,
    ts_sem,
    tr_sem,
    gs_sem,
    gr_sem,
    row_sem,
):
    me = lax.axis_index("lists")
    rep = lax.axis_index("rep")
    core = lax.rem(me, 2)
    chip = me // 2
    sibling = me + 1 - 2 * core

    def copy_to(src, dst, ssem, rsem, **device):
        return pltpu.make_async_remote_copy(
            src, dst, ssem, rsem, device_id=device, device_id_type=MESH
        )

    small_copies = [
        pltpu.make_async_copy(src, dst, in_sem.at[i])
        for i, (src, dst) in enumerate(
            ((new_hbm, new_ref), (old_hbm, old_ref), (scale_hbm, scale_ref))
        )
    ]
    for small in small_copies:
        small.start()
    pq_copy = pltpu.make_async_copy(pq_hbm, pq, pq_sem)
    pq_copy.start()
    cent_copy = pltpu.make_async_copy(
        cent_hbm.at[:, pl.ds(pl.multiple_of(rep * COLS, COLS), COLS)], cent, cent_sem
    )
    cent_copy.start()

    barrier = pltpu.get_barrier_semaphore()
    y, z = chip // 8, lax.rem(chip, 8)
    rows = [16 * wrap(y + d, 8) for d in range(8)]
    places = [2 * wrap(z + d, 8) for d in range(8)]
    for k in (2, 1, 3):
        pl.semaphore_signal(
            barrier, inc=1, device_id={"rep": lax.rem(rep + k, N_REP)}, device_id_type=MESH
        )

    for d in FAR_RING:
        for peer in (rows[d] + places[0] + core, rows[0] + places[d], rows[0] + places[d] + 1):
            pl.semaphore_signal(barrier, inc=1, device_id={"lists": peer}, device_id_type=MESH)
    pl.semaphore_signal(barrier, inc=1, device_id={"lists": sibling}, device_id_type=MESH)

    for small in small_copies:
        small.wait()
    scale = scale_ref[...].astype(F32)
    new = new_ref[...]
    owner = new // LISTS
    new_in = new - owner * LISTS + 1
    old_in = old_ref[...] - me * LISTS
    own_row = jnp.broadcast_to(owner.astype(F32), (ROWS, ROWS))
    own_col = jnp.transpose(own_row)
    earlier = (own_row == own_col) & (iota((ROWS, ROWS), 0) < iota((ROWS, ROWS), 1))
    rank = jnp.sum(jnp.where(earlier, 1.0, 0.0), axis=0, keepdims=True)
    target = owner.astype(F32) * 2.0 + rank
    new_hi = new_in // 256
    old_hi = old_in // 256
    shape = (N_REP * 32, 64)
    line = iota(shape, 0)
    pick = (line // 32) * 16 + 2 * lax.rem(line, 16) + lax.rem(line, 32) // 16
    pick = jnp.where(lax.rem(line, 16) < 8, pick, -1)
    chooser = jnp.where(pick == iota(shape, 1), 1.0, 0.0).astype(BF16)
    pq_copy.wait()
    meta = dot(chooser, pq[...].astype(F32).astype(BF16))
    line = lax.rem(iota((N_REP * 32, ROWS), 0), 32)
    extra = (
        (8, (new_in - new_hi * 256).astype(F32)),
        (24, new_hi.astype(F32)),
        (9, scale),
        (10, target),
        (11, (old_in - old_hi * 256).astype(F32)),
        (27, old_hi.astype(F32)),
    )
    for at, row in extra:
        meta = jnp.where(line == at, row, meta)
    msend[...] = meta.astype(BF16).reshape(N_REP, 32, ROWS)

    pl.semaphore_wait(barrier, N_REP - 1 + 15 + 7)
    for d in FAR_RING:
        column_peer = rows[d] + places[0] + core
        pl.semaphore_signal(row_sem, inc=1, device_id={"lists": column_peer}, device_id_type=MESH)

    for k in (2, 1, 3):
        peer = lax.rem(rep + k, N_REP)
        copy_to(msend.at[peer], mrecv.at[rep], ms_sem, mr_sem, rep=peer).start()
    for k in (2, 1, 3):
        peer = lax.rem(rep + k, N_REP)
        copy_to(
            codes_hbm.at[:, pl.ds(pl.multiple_of(peer * COLS, COLS), COLS)],
            xbuf.at[rep],
            xs_sem,
            xr_sem,
            rep=peer,
        ).start()
    own = pltpu.make_async_copy(
        codes_hbm.at[:, pl.ds(pl.multiple_of(rep * COLS, COLS), COLS)], xbuf.at[rep], loc_sem
    )
    own.start()
    mrecv[rep] = msend[rep]
    peer = lax.rem(rep + 1, N_REP)
    three = mrecv.at[pl.ds(0, N_REP - 1)]
    wait = copy_to(three, three, ms_sem, mr_sem, rep=peer)
    wait.wait_recv()
    wait.wait_send()

    low = jnp.concatenate([mrecv[s, 0:16, :] for s in range(N_REP)], axis=1).astype(F32)
    high = jnp.concatenate([mrecv[s, 16:32, :] for s in range(N_REP)], axis=1).astype(F32)
    target = low[10:11, :].astype(I32)
    owner = target // 2
    slot = (iota((1, GROUP), 1) // ROWS) * 2 + target - owner * 2
    at_owner = jnp.where(iota((N_LISTS, GROUP), 0) == owner, 1.0, 0.0).astype(BF16)
    slot_b = jnp.broadcast_to(slot, (KK, GROUP))
    low_s = jnp.concatenate([jnp.where(slot_b == q, low, 0.0) for q in range(SLOTS)], axis=0)
    high_s = jnp.concatenate([jnp.where(slot_b == q, high, 0.0) for q in range(SLOTS)], axis=0)
    routed = dot(at_owner, low_s.astype(BF16), NT) + 256.0 * dot(
        at_owner, high_s.astype(BF16), NT
    )
    esend[...] = routed.reshape(N_LISTS, 1, SLOTS * KK)

    def send_meta(peer, step):
        place = NEAR_FIRST.index(step)
        copy_to(
            esend.at[peer],
            erecv.at[2 * place + core],
            es_sem,
            er_sem.at[2 * place // HALF],
            lists=peer,
        ).start()

    pl.semaphore_wait(row_sem, 7)
    for dy, dz in FAR_FIRST:
        send_meta(rows[dy] + places[dz], (dy, dz))
        send_meta(rows[dy] + places[dz] + 1, (dy, dz))
    send_meta(sibling, (0, 0))
    erecv[core] = esend[me]

    own.wait()
    three = xbuf.at[pl.ds(0, N_REP - 1)]
    wait = copy_to(three, three, xs_sem, xr_sem, rep=peer)
    wait.wait_recv()
    wait.wait_send()
    place = owner * SLOTS + slot
    x = xbuf[...].reshape(GROUP, COLS)
    move = jnp.where(iota((N_LISTS * SLOTS, GROUP), 0) == place, 1.0, 0.0).astype(BF16)
    moved = dot(move, x).reshape(N_LISTS, SLOTS, COLS)
    vsend[...] = jnp.concatenate([moved[:, :, 0:128], moved[:, :, 128:256]], axis=1).astype(BF16)

    def send_vec(peer, step):
        place = NEAR_FIRST.index(step)
        copy_to(
            vsend.at[peer], vrecv.at[2 * place + core], vs_sem, vr_sem, lists=peer
        ).start()

    def send_vecs(first, last):
        for dy, dz in SPREAD[first:last]:
            send_vec(rows[dy] + places[dz], (dy, dz))
            send_vec(rows[dy] + places[dz] + 1, (dy, dz))

    send_vec(sibling, (0, 0))
    send_vecs(0, V1)
    vrecv[core] = vsend[me]

    scale = low[9:10, :]
    old_in = low[11:12, :] + 256.0 * high[11:12, :]
    weight = jnp.where(iota((LISTS, GROUP), 0).astype(F32) == old_in, scale, 0.0).astype(BF16)
    delta_acc[...] = dot(weight, x)
    pqk[0:8, 0:GROUP] = low[0:8, :]
    pqk[8:16, 0:GROUP] = high[0:8, :]
    lane_sub = iota((KSUB, 128), 1) // 16
    code = iota((KSUB, GROUP), 0).astype(F32).astype(BF16)
    scale_b = jnp.broadcast_to(scale.astype(BF16), (KSUB, GROUP))
    none = jnp.zeros((), BF16)

    def code_sums(hits_of, half, cols, dims):
        total = jnp.zeros((KSUB, 128), F32)
        for first in range(0, 8, STACK):
            these = range(first, first + STACK)
            hits = [hits_of((i // 4) * 8 + half * 4 + i % 4) for i in these]
            sums = dot(jnp.concatenate(hits, axis=0), cols, dims)
            for at, i in enumerate(these):
                own = lane_sub == 2 * (i % 4) + i // 4
                total = jnp.where(own, sums[at * KSUB : (at + 1) * KSUB, :], total)
        return total

    for half in range(2):
        cols = x[:, half * 128 : (half + 1) * 128]

        def value_hits(row):
            return jnp.where(code == pqk[row : row + 1, 0:GROUP].astype(BF16), scale_b, none)

        book[half * KSUB : (half + 1) * KSUB, :] = code_sums(value_hits, half, cols, NN)

    cent_copy.wait()
    eye = jnp.where(iota((COLS, COLS), 0) == iota((COLS, COLS), 1), 1.0, 0.0).astype(BF16)
    cent_t = dot(eye, cent[...], NT).astype(BF16)

    code = iota((KSUB, HALF * SLOTS), 0).astype(F32).astype(BF16)
    one = jnp.ones((), BF16)

    def unpack(part):
        held = erecv[part * HALF : (part + 1) * HALF].reshape(HALF, SLOTS * KK)
        held = jnp.concatenate([held, pltpu.roll(held, SLOTS * KK - KK, 1)], axis=0)
        got = jnp.transpose(held)
        new_rows = []
        scale_rows = []
        for q in range(0, SLOTS, 2):
            pairs = got[q * KK : q * KK + 8, :]
            odd = jnp.floor(pairs * (1.0 / 256.0))
            at = part * HALF * SLOTS + q * HALF
            pqk[0:8, at : at + 128] = pairs - 256.0 * odd
            pqk[8:16, at : at + 128] = odd
            new_rows.append(got[q * KK + 8 : q * KK + 9, :])
            scale_rows.append(got[q * KK + 9 : q * KK + 10, :])
        new_in = jnp.concatenate(new_rows, axis=1) - 1.0
        inside = iota((LISTS, HALF * SLOTS), 0).astype(F32) == new_in
        centg[part] = dot(cent_t, jnp.where(inside, 1.0, 0.0).astype(BF16)).astype(BF16)
        return inside, jnp.concatenate(scale_rows, axis=1)

    def cent_sums(part, half):
        lanes = slice(part * HALF * SLOTS, (part + 1) * HALF * SLOTS)

        def cent_hits(row):
            return jnp.where(code == pqk[row : row + 1, lanes].astype(BF16), one, none)

        return code_sums(cent_hits, half, centg[part, half * 128 : (half + 1) * 128, :], NT)

    most = erecv.at[pl.ds(0, HALF - 1)]
    copy_to(most, most, es_sem, er_sem.at[0], lists=sibling).wait_recv()
    near_inside, near_scale = unpack(0)
    for half in range(2):
        at = slice(half * KSUB, (half + 1) * KSUB)
        book[at, :] = book[at, :] - cent_sums(0, half)
    send_vecs(V1, V2)
    most = erecv.at[pl.ds(HALF, HALF)]
    copy_to(most, most, es_sem, er_sem.at[1], lists=sibling).wait_recv()
    far_inside, far_scale = unpack(1)
    pairs = []
    for half in range(2):
        total = cent_sums(1, half)
        part = pl.ds(half * 16, 16)
        comb[part] = (book[half * KSUB : (half + 1) * KSUB, :] - total).reshape(16, 2, 8, 128)
        pair = copy_to(
            comb.at[part, 1 - core], sib.at[part], bs_sem.at[half], br_sem.at[half], lists=sibling
        )
        pair.start()
        pairs.append(pair)

    block = z // 4

    def send_tiles(half):
        def send_tile(dy, near):
            row = wrap(y + dy, 8)
            place = 2 * lax.rem(row + half, 2) + core
            ahead = wrap(place - z + 8, 8)
            close = (ahead <= 2) | (ahead >= 6)
            col = jnp.where(close, 1 - near, near)
            there = row * 8 + 4 * col + place

            @pl.when(there != chip)
            def _():
                copy_to(
                    sib.at[half * 16 + row * 2 + col],
                    rsbuf.at[chip],
                    rs_sem,
                    rr_sem,
                    lists=2 * there + core,
                ).start()

        far_first = [(dy, near) for dy in range(8) for near in range(2)]
        for dy, near in sorted(far_first, key=lambda d: 2 * d[1] - hops(d[0])):
            send_tile(dy, near)

    for half in range(2):
        part = pl.ds(half * 16, 16)
        pairs[half].wait()
        sib[part] = sib[part] + comb[part, core]
        send_tiles(half)
    send_vecs(V2, V3)
    mine = lax.rem(y + z // 2, 2) * 16 + y * 2 + block
    sums_here = lax.rem(z, 2) == core

    @pl.when(sums_here)
    def _():
        rsbuf[chip] = sib[mine]
        most = rsbuf.at[pl.ds(0, CHIPS - 1)]
        copy_to(most, most, rs_sem, rr_sem, lists=sibling).wait_recv()
        total = jnp.sum(rsbuf[...], axis=0)
        shift = lax.rem(iota((8, 128), 1) // 16 - iota((8, 128), 0) + 8, 8)
        turned = total
        for d in range(1, 8):
            moved = pltpu.roll(pltpu.roll(total, 8 - d, 0), 16 * d, 1)
            turned = jnp.where(shift == d, moved, turned)
        tile[...] = turned
        gathered[core, mine] = turned

        def send_sum(peer):
            copy_to(
                tile, gathered.at[core, mine], gs_sem, gr_sem, lists=peer
            ).start()

        for dy, dz in FAR_FIRST:
            send_sum(rows[dy] + places[dz] + core)

    most = erecv.at[pl.ds(0, N_LISTS - 1)]
    copy_to(most, most, es_sem, er_sem.at[0], lists=sibling).wait_send()

    most = vrecv.at[pl.ds(0, N_LISTS - 1)]
    wait = copy_to(most, most, vs_sem, vr_sem, lists=sibling)
    wait.wait_recv()
    wait.wait_send()
    vflat[...] = vrecv[...].astype(F32).reshape(N_LISTS * 16, 128)
    vecs = jnp.concatenate(
        [
            jnp.concatenate(
                [
                    vflat[pl.ds(part * HALF * 16 + h * 8 + q, HALF, stride=16), :].astype(BF16)
                    for h in range(2)
                ],
                axis=1,
            )
            for part in range(2)
            for q in range(SLOTS)
        ],
        axis=0,
    )
    weight = jnp.concatenate(
        [jnp.where(near_inside, near_scale, 0.0), jnp.where(far_inside, far_scale, 0.0)], axis=1
    ).astype(BF16)
    delta_out[...] = (dot(weight, vecs) - delta_acc[...]).astype(BF16)

    @pl.when(sums_here)
    def _():
        most = gathered.at[core, pl.ds(0, CHIPS // 2 - 1)]
        copy_to(most, most, gs_sem, gr_sem, lists=sibling).wait_recv()

    @pl.when(jnp.logical_not(sums_here))
    def _():
        most = gathered.at[core]
        copy_to(most, most, gs_sem, gr_sem, lists=sibling).wait_recv()

    give = copy_to(gathered.at[core], gathered.at[core], ts_sem, tr_sem, lists=sibling)
    give.start()

    @pl.when(sums_here)
    def _():
        most = rsbuf.at[pl.ds(0, CHIPS - 1)]
        copy_to(most, most, gs_sem, gr_sem, lists=sibling).wait_send()
        most = sib.at[pl.ds(0, CHIPS // 2 - 1)]
        copy_to(most, most, rs_sem, rr_sem, lists=sibling).wait_send()

    @pl.when(jnp.logical_not(sums_here))
    def _():
        copy_to(sib, sib, rs_sem, rr_sem, lists=sibling).wait_send()

    give.wait()
    for t in range(CHIPS):
        half, block = t // 32, t % 32
        book_out[half * 8 : half * 8 + 8, block * 128 : (block + 1) * 128] = gathered[
            t % 2, t // 2
        ]


def body(vector_codes, row_scales, old_list, new_list, pq_codes, centroids):
    vmem = pl.BlockSpec(memory_space=pltpu.VMEM)
    hbm = pl.BlockSpec(memory_space=pltpu.HBM)
    return pl.pallas_call(
        kernel,
        name="rebuild_window",
        out_shape=(
            pltpu.VMEM((LISTS, COLS), BF16),
            pltpu.VMEM((16, 4096), F32),
        ),
        in_specs=[hbm] * 6,
        out_specs=(vmem, vmem),
        scratch_shapes=[
            pltpu.VMEM((1, ROWS), BF16),
            pltpu.VMEM((1, ROWS), I32),
            pltpu.VMEM((1, ROWS), I32),
            pltpu.VMEM((64, ROWS), I32),
            pltpu.VMEM((LISTS, COLS), BF16),
            pltpu.VMEM((N_REP, ROWS, COLS), BF16),
            pltpu.VMEM((N_REP, 32, ROWS), BF16),
            pltpu.VMEM((N_REP, 32, ROWS), BF16),
            pltpu.VMEM((N_LISTS, 1, 128), F32),
            pltpu.VMEM((N_LISTS, 1, 128), F32),
            pltpu.VMEM((N_LISTS, 16, 128), BF16),
            pltpu.VMEM((N_LISTS, 16, 128), BF16),
            pltpu.VMEM((LISTS, COLS), F32),
            pltpu.VMEM((N_LISTS * 16, 128), F32),
            pltpu.VMEM((16, N_LISTS * SLOTS), F32),
            pltpu.VMEM((2, COLS, HALF * SLOTS), BF16),
            pltpu.VMEM((2 * KSUB, 128), F32),
            pltpu.VMEM((CHIPS // 2, 8, 128), F32),
            pltpu.VMEM((CHIPS // 2, 2, 8, 128), F32),
            pltpu.VMEM((CHIPS, 8, 128), F32),
            pltpu.VMEM((8, 128), F32),
            pltpu.VMEM((2, CHIPS // 2, 8, 128), F32),
        ]
        + [pltpu.SemaphoreType.DMA((3,))]
        + [pltpu.SemaphoreType.DMA] * 8
        + [pltpu.SemaphoreType.DMA((2,))]
        + [pltpu.SemaphoreType.DMA] * 2
        + [pltpu.SemaphoreType.DMA((2,))] * 2
        + [pltpu.SemaphoreType.DMA] * 6
        + [pltpu.SemaphoreType.REGULAR],
        compiler_params=pltpu.CompilerParams(
            collective_id=0, has_side_effects=True, vmem_limit_bytes=56 * 1024 * 1024
        ),
    )(
        vector_codes,
        row_scales.reshape(1, ROWS),
        old_list.reshape(1, ROWS),
        new_list.reshape(1, ROWS),
        pq_codes.T,
        centroids,
    )


def solution(mesh):
    return jax.shard_map(
        body,
        mesh=mesh,
        in_specs=(
            P(("lists", "rep"), None),
            P(("lists", "rep")),
            P(("lists", "rep")),
            P(("lists", "rep")),
            P(("lists", "rep"), None),
            P("lists", None),
        ),
        out_specs=(P("lists", "rep"), P("rep", None)),
        check_vma=False,
    )
```

```python
import functools

import jax
import jax.numpy as jnp
from jax import lax
from jax.experimental import pallas as pl
from jax.experimental.pallas import tpu as pltpu
from jax.sharding import PartitionSpec as P

MESH = pl.DeviceIdType.MESH
F32 = jnp.float32
BF16 = jnp.bfloat16
I32 = jnp.int32

N_LISTS = 128
N_REP = 4
CHIPS = N_LISTS // 2
ROWS = 128
GROUP = ROWS * N_REP
LISTS = 512
COLS = 256
SLOTS = 8
KK = 16
KSUB = 256
STACK = 4
V1, V2, V3 = 36, 36, 63
NT = (((1,), (1,)), ((), ()))
NN = (((1,), (0,)), ((), ()))


def dot(a, b, dims=NN):
    return lax.dot_general(a, b, dims, preferred_element_type=F32)


def iota(shape, axis):
    return lax.broadcasted_iota(I32, shape, axis)


def wrap(value, size):
    return jnp.where(value >= size, value - size, value)


def hops(step):
    return min(step, 8 - step)


NEAR_FIRST = sorted(
    ((dy, dz) for dy in range(8) for dz in range(8)), key=lambda d: hops(d[0]) + hops(d[1])
)
FAR_FIRST = NEAR_FIRST[:0:-1]
SPREAD = [(k * 27 % CHIPS // 8, k * 27 % 8) for k in range(1, CHIPS)]
HALF = N_LISTS // 2
FAR_RING = sorted(range(1, 8), key=lambda d: -hops(d))


def kernel(
    codes_hbm,
    scale_hbm,
    old_hbm,
    new_hbm,
    pq_hbm,
    cent_hbm,
    delta_out,
    book_out,
    scale_ref,
    old_ref,
    new_ref,
    pq,
    cent,
    xbuf,
    msend,
    mrecv,
    esend,
    erecv,
    vsend,
    vrecv,
    delta_acc,
    vflat,
    pqk,
    centg,
    book,
    sib,
    comb,
    rsbuf,
    tile,
    gathered,
    in_sem,
    pq_sem,
    cent_sem,
    loc_sem,
    xs_sem,
    xr_sem,
    ms_sem,
    mr_sem,
    es_sem,
    er_sem,
    vs_sem,
    vr_sem,
    bs_sem,
    br_sem,
    rs_sem,
    rr_sem,
    ts_sem,
    tr_sem,
    gs_sem,
    gr_sem,
    row_sem,
):
    me = lax.axis_index("lists")
    rep = lax.axis_index("rep")
    core = lax.rem(me, 2)
    chip = me // 2
    sibling = me + 1 - 2 * core

    def copy_to(src, dst, ssem, rsem, **device):
        return pltpu.make_async_remote_copy(
            src, dst, ssem, rsem, device_id=device, device_id_type=MESH
        )

    small_copies = [
        pltpu.make_async_copy(src, dst, in_sem.at[i])
        for i, (src, dst) in enumerate(
            ((new_hbm, new_ref), (old_hbm, old_ref), (scale_hbm, scale_ref))
        )
    ]
    for small in small_copies:
        small.start()
    pq_copy = pltpu.make_async_copy(pq_hbm, pq, pq_sem)
    pq_copy.start()
    cent_copy = pltpu.make_async_copy(
        cent_hbm.at[:, pl.ds(pl.multiple_of(rep * COLS, COLS), COLS)], cent, cent_sem
    )
    cent_copy.start()

    barrier = pltpu.get_barrier_semaphore()
    y, z = chip // 8, lax.rem(chip, 8)
    rows = [16 * wrap(y + d, 8) for d in range(8)]
    places = [2 * wrap(z + d, 8) for d in range(8)]
    for k in (2, 1, 3):
        pl.semaphore_signal(
            barrier, inc=1, device_id={"rep": lax.rem(rep + k, N_REP)}, device_id_type=MESH
        )

    for d in FAR_RING:
        for peer in (rows[d] + places[0] + core, rows[0] + places[d], rows[0] + places[d] + 1):
            pl.semaphore_signal(barrier, inc=1, device_id={"lists": peer}, device_id_type=MESH)
    pl.semaphore_signal(barrier, inc=1, device_id={"lists": sibling}, device_id_type=MESH)

    for small in small_copies:
        small.wait()
    scale = scale_ref[...].astype(F32)
    new = new_ref[...]
    owner = new // LISTS
    new_in = new - owner * LISTS + 1
    old_in = old_ref[...] - me * LISTS
    own_row = jnp.broadcast_to(owner.astype(F32), (ROWS, ROWS))
    own_col = jnp.transpose(own_row)
    earlier = (own_row == own_col) & (iota((ROWS, ROWS), 0) < iota((ROWS, ROWS), 1))
    rank = jnp.sum(jnp.where(earlier, 1.0, 0.0), axis=0, keepdims=True)
    target = owner.astype(F32) * 2.0 + rank
    new_hi = new_in // 256
    old_hi = old_in // 256
    shape = (N_REP * 32, 64)
    line = iota(shape, 0)
    pick = (line // 32) * 16 + 2 * lax.rem(line, 16) + lax.rem(line, 32) // 16
    pick = jnp.where(lax.rem(line, 16) < 8, pick, -1)
    chooser = jnp.where(pick == iota(shape, 1), 1.0, 0.0).astype(BF16)
    pq_copy.wait()
    meta = dot(chooser, pq[...].astype(F32).astype(BF16))
    line = lax.rem(iota((N_REP * 32, ROWS), 0), 32)
    extra = (
        (8, (new_in - new_hi * 256).astype(F32)),
        (24, new_hi.astype(F32)),
        (9, scale),
        (10, target),
        (11, (old_in - old_hi * 256).astype(F32)),
        (27, old_hi.astype(F32)),
    )
    for at, row in extra:
        meta = jnp.where(line == at, row, meta)
    msend[...] = meta.astype(BF16).reshape(N_REP, 32, ROWS)

    pl.semaphore_wait(barrier, N_REP - 1 + 15 + 7)
    for d in FAR_RING:
        column_peer = rows[d] + places[0] + core
        pl.semaphore_signal(row_sem, inc=1, device_id={"lists": column_peer}, device_id_type=MESH)

    for k in (2, 1, 3):
        peer = lax.rem(rep + k, N_REP)
        copy_to(msend.at[peer], mrecv.at[rep], ms_sem, mr_sem, rep=peer).start()
    for k in (2, 1, 3):
        peer = lax.rem(rep + k, N_REP)
        copy_to(
            codes_hbm.at[:, pl.ds(pl.multiple_of(peer * COLS, COLS), COLS)],
            xbuf.at[rep],
            xs_sem,
            xr_sem,
            rep=peer,
        ).start()
    own = pltpu.make_async_copy(
        codes_hbm.at[:, pl.ds(pl.multiple_of(rep * COLS, COLS), COLS)], xbuf.at[rep], loc_sem
    )
    own.start()
    mrecv[rep] = msend[rep]
    peer = lax.rem(rep + 1, N_REP)
    three = mrecv.at[pl.ds(0, N_REP - 1)]
    wait = copy_to(three, three, ms_sem, mr_sem, rep=peer)
    wait.wait_recv()
    wait.wait_send()

    low = jnp.concatenate([mrecv[s, 0:16, :] for s in range(N_REP)], axis=1).astype(F32)
    high = jnp.concatenate([mrecv[s, 16:32, :] for s in range(N_REP)], axis=1).astype(F32)
    target = low[10:11, :].astype(I32)
    owner = target // 2
    slot = (iota((1, GROUP), 1) // ROWS) * 2 + target - owner * 2
    at_owner = jnp.where(iota((N_LISTS, GROUP), 0) == owner, 1.0, 0.0).astype(BF16)
    slot_b = jnp.broadcast_to(slot, (KK, GROUP))
    low_s = jnp.concatenate([jnp.where(slot_b == q, low, 0.0) for q in range(SLOTS)], axis=0)
    high_s = jnp.concatenate([jnp.where(slot_b == q, high, 0.0) for q in range(SLOTS)], axis=0)
    routed = dot(at_owner, low_s.astype(BF16), NT) + 256.0 * dot(
        at_owner, high_s.astype(BF16), NT
    )
    esend[...] = routed.reshape(N_LISTS, 1, SLOTS * KK)

    def send_meta(peer, step):
        place = NEAR_FIRST.index(step)
        copy_to(
            esend.at[peer],
            erecv.at[2 * place + core],
            es_sem,
            er_sem.at[2 * place // HALF],
            lists=peer,
        ).start()

    pl.semaphore_wait(row_sem, 7)
    for dy, dz in FAR_FIRST:
        send_meta(rows[dy] + places[dz], (dy, dz))
        send_meta(rows[dy] + places[dz] + 1, (dy, dz))
    send_meta(sibling, (0, 0))
    erecv[core] = esend[me]

    own.wait()
    three = xbuf.at[pl.ds(0, N_REP - 1)]
    wait = copy_to(three, three, xs_sem, xr_sem, rep=peer)
    wait.wait_recv()
    wait.wait_send()
    place = owner * SLOTS + slot
    x = xbuf[...].reshape(GROUP, COLS)
    move = jnp.where(iota((N_LISTS * SLOTS, GROUP), 0) == place, 1.0, 0.0).astype(BF16)
    moved = dot(move, x).reshape(N_LISTS, SLOTS, COLS)
    vsend[...] = jnp.concatenate([moved[:, :, 0:128], moved[:, :, 128:256]], axis=1).astype(BF16)

    def send_vec(peer, step):
        place = NEAR_FIRST.index(step)
        copy_to(
            vsend.at[peer], vrecv.at[2 * place + core], vs_sem, vr_sem, lists=peer
        ).start()

    def send_vecs(first, last):
        for dy, dz in SPREAD[first:last]:
            send_vec(rows[dy] + places[dz], (dy, dz))
            send_vec(rows[dy] + places[dz] + 1, (dy, dz))

    send_vec(sibling, (0, 0))
    send_vecs(0, V1)
    vrecv[core] = vsend[me]

    scale = low[9:10, :]
    old_in = low[11:12, :] + 256.0 * high[11:12, :]
    weight = jnp.where(iota((LISTS, GROUP), 0).astype(F32) == old_in, scale, 0.0).astype(BF16)
    delta_acc[...] = dot(weight, x)
    pqk[0:8, 0:GROUP] = low[0:8, :]
    pqk[8:16, 0:GROUP] = high[0:8, :]
    lane_sub = iota((KSUB, 128), 1) // 16
    code = iota((KSUB, GROUP), 0).astype(F32).astype(BF16)
    scale_b = jnp.broadcast_to(scale.astype(BF16), (KSUB, GROUP))
    none = jnp.zeros((), BF16)

    def code_sums(hits_of, half, cols, dims):
        total = jnp.zeros((KSUB, 128), F32)
        for first in range(0, 8, STACK):
            these = range(first, first + STACK)
            hits = [hits_of((i // 4) * 8 + half * 4 + i % 4) for i in these]
            sums = dot(jnp.concatenate(hits, axis=0), cols, dims)
            for at, i in enumerate(these):
                own = lane_sub == 2 * (i % 4) + i // 4
                total = jnp.where(own, sums[at * KSUB : (at + 1) * KSUB, :], total)
        return total

    for half in range(2):
        cols = x[:, half * 128 : (half + 1) * 128]

        def value_hits(row):
            return jnp.where(code == pqk[row : row + 1, 0:GROUP].astype(BF16), scale_b, none)

        book[half * KSUB : (half + 1) * KSUB, :] = code_sums(value_hits, half, cols, NN)

    cent_copy.wait()
    eye = jnp.where(iota((COLS, COLS), 0) == iota((COLS, COLS), 1), 1.0, 0.0).astype(BF16)
    cent_t = dot(eye, cent[...], NT).astype(BF16)

    code = iota((KSUB, HALF * SLOTS), 0).astype(F32).astype(BF16)
    one = jnp.ones((), BF16)

    def unpack(part):
        held = erecv[part * HALF : (part + 1) * HALF].reshape(HALF, SLOTS * KK)
        held = jnp.concatenate([held, pltpu.roll(held, SLOTS * KK - KK, 1)], axis=0)
        got = jnp.transpose(held)
        new_rows = []
        scale_rows = []
        for q in range(0, SLOTS, 2):
            pairs = got[q * KK : q * KK + 8, :]
            odd = jnp.floor(pairs * (1.0 / 256.0))
            at = part * HALF * SLOTS + q * HALF
            pqk[0:8, at : at + 128] = pairs - 256.0 * odd
            pqk[8:16, at : at + 128] = odd
            new_rows.append(got[q * KK + 8 : q * KK + 9, :])
            scale_rows.append(got[q * KK + 9 : q * KK + 10, :])
        new_in = jnp.concatenate(new_rows, axis=1) - 1.0
        inside = iota((LISTS, HALF * SLOTS), 0).astype(F32) == new_in
        centg[part] = dot(cent_t, jnp.where(inside, 1.0, 0.0).astype(BF16)).astype(BF16)
        return inside, jnp.concatenate(scale_rows, axis=1)

    def cent_sums(part, half):
        lanes = slice(part * HALF * SLOTS, (part + 1) * HALF * SLOTS)

        def cent_hits(row):
            return jnp.where(code == pqk[row : row + 1, lanes].astype(BF16), one, none)

        return code_sums(cent_hits, half, centg[part, half * 128 : (half + 1) * 128, :], NT)

    most = erecv.at[pl.ds(0, HALF - 1)]
    copy_to(most, most, es_sem, er_sem.at[0], lists=sibling).wait_recv()
    near_inside, near_scale = unpack(0)
    for half in range(2):
        at = slice(half * KSUB, (half + 1) * KSUB)
        book[at, :] = book[at, :] - cent_sums(0, half)
    send_vecs(V1, V2)
    most = erecv.at[pl.ds(HALF, HALF)]
    copy_to(most, most, es_sem, er_sem.at[1], lists=sibling).wait_recv()
    far_inside, far_scale = unpack(1)
    pairs = []
    for half in range(2):
        total = cent_sums(1, half)
        part = pl.ds(half * 16, 16)
        comb[part] = (book[half * KSUB : (half + 1) * KSUB, :] - total).reshape(16, 2, 8, 128)
        pair = copy_to(
            comb.at[part, 1 - core], sib.at[part], bs_sem.at[half], br_sem.at[half], lists=sibling
        )
        pair.start()
        pairs.append(pair)

    block = z // 4

    def send_tiles(half):
        def send_tile(dy, near):
            row = wrap(y + dy, 8)
            place = 2 * lax.rem(row + half, 2) + core
            ahead = wrap(place - z + 8, 8)
            close = (ahead <= 2) | (ahead >= 6)
            col = jnp.where(close, 1 - near, near)
            there = row * 8 + 4 * col + place

            @pl.when(there != chip)
            def _():
                copy_to(
                    sib.at[half * 16 + row * 2 + col],
                    rsbuf.at[chip],
                    rs_sem,
                    rr_sem,
                    lists=2 * there + core,
                ).start()

        far_first = [(dy, near) for dy in range(8) for near in range(2)]
        for dy, near in sorted(far_first, key=lambda d: 2 * d[1] - hops(d[0])):
            send_tile(dy, near)

    for half in range(2):
        part = pl.ds(half * 16, 16)
        pairs[half].wait()
        sib[part] = sib[part] + comb[part, core]
        send_tiles(half)
    send_vecs(V2, V3)
    mine = lax.rem(y + z // 2, 2) * 16 + y * 2 + block
    sums_here = lax.rem(z, 2) == core

    @pl.when(sums_here)
    def _():
        rsbuf[chip] = sib[mine]
        most = rsbuf.at[pl.ds(0, CHIPS - 1)]
        copy_to(most, most, rs_sem, rr_sem, lists=sibling).wait_recv()
        total = jnp.sum(rsbuf[...], axis=0)
        shift = lax.rem(iota((8, 128), 1) // 16 - iota((8, 128), 0) + 8, 8)
        turned = total
        for d in range(1, 8):
            moved = pltpu.roll(pltpu.roll(total, 8 - d, 0), 16 * d, 1)
            turned = jnp.where(shift == d, moved, turned)
        tile[...] = turned
        gathered[core, mine] = turned

        def send_sum(peer):
            copy_to(
                tile, gathered.at[core, mine], gs_sem, gr_sem, lists=peer
            ).start()

        for dy, dz in FAR_FIRST:
            send_sum(rows[dy] + places[dz] + core)

    most = erecv.at[pl.ds(0, N_LISTS - 1)]
    copy_to(most, most, es_sem, er_sem.at[0], lists=sibling).wait_send()

    most = vrecv.at[pl.ds(0, N_LISTS - 1)]
    wait = copy_to(most, most, vs_sem, vr_sem, lists=sibling)
    wait.wait_recv()
    wait.wait_send()
    vflat[...] = vrecv[...].astype(F32).reshape(N_LISTS * 16, 128)
    vecs = jnp.concatenate(
        [
            jnp.concatenate(
                [
                    vflat[pl.ds(part * HALF * 16 + h * 8 + q, HALF, stride=16), :].astype(BF16)
                    for h in range(2)
                ],
                axis=1,
            )
            for part in range(2)
            for q in range(SLOTS)
        ],
        axis=0,
    )
    weight = jnp.concatenate(
        [jnp.where(near_inside, near_scale, 0.0), jnp.where(far_inside, far_scale, 0.0)], axis=1
    ).astype(BF16)
    delta_out[...] = (dot(weight, vecs) - delta_acc[...]).astype(BF16)

    @pl.when(sums_here)
    def _():
        most = gathered.at[core, pl.ds(0, CHIPS // 2 - 1)]
        copy_to(most, most, gs_sem, gr_sem, lists=sibling).wait_recv()

    @pl.when(jnp.logical_not(sums_here))
    def _():
        most = gathered.at[core]
        copy_to(most, most, gs_sem, gr_sem, lists=sibling).wait_recv()

    give = copy_to(gathered.at[core], gathered.at[core], ts_sem, tr_sem, lists=sibling)
    give.start()

    @pl.when(sums_here)
    def _():
        most = rsbuf.at[pl.ds(0, CHIPS - 1)]
        copy_to(most, most, gs_sem, gr_sem, lists=sibling).wait_send()
        most = sib.at[pl.ds(0, CHIPS // 2 - 1)]
        copy_to(most, most, rs_sem, rr_sem, lists=sibling).wait_send()

    @pl.when(jnp.logical_not(sums_here))
    def _():
        copy_to(sib, sib, rs_sem, rr_sem, lists=sibling).wait_send()

    give.wait()
    for t in range(CHIPS):
        half, block = t // 32, t % 32
        book_out[half * 8 : half * 8 + 8, block * 128 : (block + 1) * 128] = gathered[
            t % 2, t // 2
        ]


def body(vector_codes, row_scales, old_list, new_list, pq_codes, centroids):
    vmem = pl.BlockSpec(memory_space=pltpu.VMEM)
    hbm = pl.BlockSpec(memory_space=pltpu.HBM)
    return pl.pallas_call(
        kernel,
        name="rebuild_window",
        out_shape=(
            pltpu.VMEM((LISTS, COLS), BF16),
            pltpu.VMEM((16, 4096), F32),
        ),
        in_specs=[hbm] * 6,
        out_specs=(vmem, vmem),
        scratch_shapes=[
            pltpu.VMEM((1, ROWS), BF16),
            pltpu.VMEM((1, ROWS), I32),
            pltpu.VMEM((1, ROWS), I32),
            pltpu.VMEM((64, ROWS), I32),
            pltpu.VMEM((LISTS, COLS), BF16),
            pltpu.VMEM((N_REP, ROWS, COLS), BF16),
            pltpu.VMEM((N_REP, 32, ROWS), BF16),
            pltpu.VMEM((N_REP, 32, ROWS), BF16),
            pltpu.VMEM((N_LISTS, 1, 128), F32),
            pltpu.VMEM((N_LISTS, 1, 128), F32),
            pltpu.VMEM((N_LISTS, 16, 128), BF16),
            pltpu.VMEM((N_LISTS, 16, 128), BF16),
            pltpu.VMEM((LISTS, COLS), F32),
            pltpu.VMEM((N_LISTS * 16, 128), F32),
            pltpu.VMEM((16, N_LISTS * SLOTS), F32),
            pltpu.VMEM((2, COLS, HALF * SLOTS), BF16),
            pltpu.VMEM((2 * KSUB, 128), F32),
            pltpu.VMEM((CHIPS // 2, 8, 128), F32),
            pltpu.VMEM((CHIPS // 2, 2, 8, 128), F32),
            pltpu.VMEM((CHIPS, 8, 128), F32),
            pltpu.VMEM((8, 128), F32),
            pltpu.VMEM((2, CHIPS // 2, 8, 128), F32),
        ]
        + [pltpu.SemaphoreType.DMA((3,))]
        + [pltpu.SemaphoreType.DMA] * 8
        + [pltpu.SemaphoreType.DMA((2,))]
        + [pltpu.SemaphoreType.DMA] * 2
        + [pltpu.SemaphoreType.DMA((2,))] * 2
        + [pltpu.SemaphoreType.DMA] * 6
        + [pltpu.SemaphoreType.REGULAR],
        compiler_params=pltpu.CompilerParams(
            collective_id=0, has_side_effects=True, vmem_limit_bytes=56 * 1024 * 1024
        ),
    )(
        vector_codes,
        row_scales.reshape(1, ROWS),
        old_list.reshape(1, ROWS),
        new_list.reshape(1, ROWS),
        pq_codes.T,
        centroids,
    )


def solution(mesh):
    return jax.shard_map(
        body,
        mesh=mesh,
        in_specs=(
            P(("lists", "rep"), None),
            P(("lists", "rep")),
            P(("lists", "rep")),
            P(("lists", "rep")),
            P(("lists", "rep"), None),
            P("lists", None),
        ),
        out_specs=(P("lists", "rep"), P("rep", None)),
        check_vma=False,
    )
```

```python
import functools

import jax
import jax.numpy as jnp
from jax import lax
from jax.experimental import pallas as pl
from jax.experimental.pallas import tpu as pltpu
from jax.sharding import PartitionSpec as P

MESH = pl.DeviceIdType.MESH
F32 = jnp.float32
BF16 = jnp.bfloat16
I32 = jnp.int32

N_LISTS = 128
N_REP = 4
CHIPS = N_LISTS // 2
ROWS = 128
GROUP = ROWS * N_REP
LISTS = 512
COLS = 256
SLOTS = 8
KK = 16
KSUB = 256
STACK = 4
V1, V2, V3 = 36, 36, 63
NT = (((1,), (1,)), ((), ()))
NN = (((1,), (0,)), ((), ()))


def dot(a, b, dims=NN):
    return lax.dot_general(a, b, dims, preferred_element_type=F32)


def iota(shape, axis):
    return lax.broadcasted_iota(I32, shape, axis)


def wrap(value, size):
    return jnp.where(value >= size, value - size, value)


def hops(step):
    return min(step, 8 - step)


NEAR_FIRST = sorted(
    ((dy, dz) for dy in range(8) for dz in range(8)), key=lambda d: hops(d[0]) + hops(d[1])
)
FAR_FIRST = NEAR_FIRST[:0:-1]
SPREAD = [(k * 27 % CHIPS // 8, k * 27 % 8) for k in range(1, CHIPS)]
HALF = N_LISTS // 2
FAR_RING = sorted(range(1, 8), key=lambda d: -hops(d))


def kernel(
    codes_hbm,
    scale_hbm,
    old_hbm,
    new_hbm,
    pq_hbm,
    cent_hbm,
    delta_out,
    book_out,
    scale_ref,
    old_ref,
    new_ref,
    pq,
    cent,
    xbuf,
    msend,
    mrecv,
    esend,
    erecv,
    vsend,
    vrecv,
    delta_acc,
    vflat,
    pqk,
    centg,
    book,
    sib,
    comb,
    rsbuf,
    tile,
    gathered,
    in_sem,
    pq_sem,
    cent_sem,
    loc_sem,
    xs_sem,
    xr_sem,
    ms_sem,
    mr_sem,
    es_sem,
    er_sem,
    vs_sem,
    vr_sem,
    bs_sem,
    br_sem,
    rs_sem,
    rr_sem,
    ts_sem,
    tr_sem,
    gs_sem,
    gr_sem,
    row_sem,
):
    me = lax.axis_index("lists")
    rep = lax.axis_index("rep")
    core = lax.rem(me, 2)
    chip = me // 2
    sibling = me + 1 - 2 * core

    def copy_to(src, dst, ssem, rsem, **device):
        return pltpu.make_async_remote_copy(
            src, dst, ssem, rsem, device_id=device, device_id_type=MESH
        )

    small_copies = [
        pltpu.make_async_copy(src, dst, in_sem.at[i])
        for i, (src, dst) in enumerate(
            ((new_hbm, new_ref), (old_hbm, old_ref), (scale_hbm, scale_ref))
        )
    ]
    for small in small_copies:
        small.start()
    pq_copy = pltpu.make_async_copy(pq_hbm, pq, pq_sem)
    pq_copy.start()
    cent_copy = pltpu.make_async_copy(
        cent_hbm.at[:, pl.ds(pl.multiple_of(rep * COLS, COLS), COLS)], cent, cent_sem
    )
    cent_copy.start()

    barrier = pltpu.get_barrier_semaphore()
    y, z = chip // 8, lax.rem(chip, 8)
    rows = [16 * wrap(y + d, 8) for d in range(8)]
    places = [2 * wrap(z + d, 8) for d in range(8)]
    for k in (2, 1, 3):
        pl.semaphore_signal(
            barrier, inc=1, device_id={"rep": lax.rem(rep + k, N_REP)}, device_id_type=MESH
        )

    for d in FAR_RING:
        for peer in (rows[d] + places[0] + core, rows[0] + places[d], rows[0] + places[d] + 1):
            pl.semaphore_signal(barrier, inc=1, device_id={"lists": peer}, device_id_type=MESH)
    pl.semaphore_signal(barrier, inc=1, device_id={"lists": sibling}, device_id_type=MESH)

    for small in small_copies:
        small.wait()
    scale = scale_ref[...].astype(F32)
    new = new_ref[...]
    owner = new // LISTS
    new_in = new - owner * LISTS + 1
    old_in = old_ref[...] - me * LISTS
    own_row = jnp.broadcast_to(owner.astype(F32), (ROWS, ROWS))
    own_col = jnp.transpose(own_row)
    earlier = (own_row == own_col) & (iota((ROWS, ROWS), 0) < iota((ROWS, ROWS), 1))
    rank = jnp.sum(jnp.where(earlier, 1.0, 0.0), axis=0, keepdims=True)
    target = owner.astype(F32) * 2.0 + rank
    new_hi = new_in // 256
    old_hi = old_in // 256
    shape = (N_REP * 32, 64)
    line = iota(shape, 0)
    pick = (line // 32) * 16 + 2 * lax.rem(line, 16) + lax.rem(line, 32) // 16
    pick = jnp.where(lax.rem(line, 16) < 8, pick, -1)
    chooser = jnp.where(pick == iota(shape, 1), 1.0, 0.0).astype(BF16)
    pq_copy.wait()
    meta = dot(chooser, pq[...].astype(F32).astype(BF16))
    line = lax.rem(iota((N_REP * 32, ROWS), 0), 32)
    extra = (
        (8, (new_in - new_hi * 256).astype(F32)),
        (24, new_hi.astype(F32)),
        (9, scale),
        (10, target),
        (11, (old_in - old_hi * 256).astype(F32)),
        (27, old_hi.astype(F32)),
    )
    for at, row in extra:
        meta = jnp.where(line == at, row, meta)
    msend[...] = meta.astype(BF16).reshape(N_REP, 32, ROWS)

    pl.semaphore_wait(barrier, N_REP - 1 + 15 + 7)
    for d in FAR_RING:
        column_peer = rows[d] + places[0] + core
        pl.semaphore_signal(row_sem, inc=1, device_id={"lists": column_peer}, device_id_type=MESH)

    for k in (2, 1, 3):
        peer = lax.rem(rep + k, N_REP)
        copy_to(msend.at[peer], mrecv.at[rep], ms_sem, mr_sem, rep=peer).start()
    for k in (2, 1, 3):
        peer = lax.rem(rep + k, N_REP)
        copy_to(
            codes_hbm.at[:, pl.ds(pl.multiple_of(peer * COLS, COLS), COLS)],
            xbuf.at[rep],
            xs_sem,
            xr_sem,
            rep=peer,
        ).start()
    own = pltpu.make_async_copy(
        codes_hbm.at[:, pl.ds(pl.multiple_of(rep * COLS, COLS), COLS)], xbuf.at[rep], loc_sem
    )
    own.start()
    mrecv[rep] = msend[rep]
    peer = lax.rem(rep + 1, N_REP)
    three = mrecv.at[pl.ds(0, N_REP - 1)]
    wait = copy_to(three, three, ms_sem, mr_sem, rep=peer)
    wait.wait_recv()
    wait.wait_send()

    low = jnp.concatenate([mrecv[s, 0:16, :] for s in range(N_REP)], axis=1).astype(F32)
    high = jnp.concatenate([mrecv[s, 16:32, :] for s in range(N_REP)], axis=1).astype(F32)
    target = low[10:11, :].astype(I32)
    owner = target // 2
    slot = (iota((1, GROUP), 1) // ROWS) * 2 + target - owner * 2
    at_owner = jnp.where(iota((N_LISTS, GROUP), 0) == owner, 1.0, 0.0).astype(BF16)
    slot_b = jnp.broadcast_to(slot, (KK, GROUP))
    low_s = jnp.concatenate([jnp.where(slot_b == q, low, 0.0) for q in range(SLOTS)], axis=0)
    high_s = jnp.concatenate([jnp.where(slot_b == q, high, 0.0) for q in range(SLOTS)], axis=0)
    routed = dot(at_owner, low_s.astype(BF16), NT) + 256.0 * dot(
        at_owner, high_s.astype(BF16), NT
    )
    esend[...] = routed.reshape(N_LISTS, 1, SLOTS * KK)

    def send_meta(peer, step):
        place = NEAR_FIRST.index(step)
        copy_to(
            esend.at[peer],
            erecv.at[2 * place + core],
            es_sem,
            er_sem.at[2 * place // HALF],
            lists=peer,
        ).start()

    pl.semaphore_wait(row_sem, 7)
    for dy, dz in FAR_FIRST:
        send_meta(rows[dy] + places[dz], (dy, dz))
        send_meta(rows[dy] + places[dz] + 1, (dy, dz))
    send_meta(sibling, (0, 0))
    erecv[core] = esend[me]

    own.wait()
    three = xbuf.at[pl.ds(0, N_REP - 1)]
    wait = copy_to(three, three, xs_sem, xr_sem, rep=peer)
    wait.wait_recv()
    wait.wait_send()
    place = owner * SLOTS + slot
    x = xbuf[...].reshape(GROUP, COLS)
    move = jnp.where(iota((N_LISTS * SLOTS, GROUP), 0) == place, 1.0, 0.0).astype(BF16)
    moved = dot(move, x).reshape(N_LISTS, SLOTS, COLS)
    vsend[...] = jnp.concatenate([moved[:, :, 0:128], moved[:, :, 128:256]], axis=1).astype(BF16)

    def send_vec(peer, step):
        place = NEAR_FIRST.index(step)
        copy_to(
            vsend.at[peer], vrecv.at[2 * place + core], vs_sem, vr_sem, lists=peer
        ).start()

    def send_vecs(first, last):
        for dy, dz in SPREAD[first:last]:
            send_vec(rows[dy] + places[dz], (dy, dz))
            send_vec(rows[dy] + places[dz] + 1, (dy, dz))

    send_vec(sibling, (0, 0))
    send_vecs(0, V1)
    vrecv[core] = vsend[me]

    scale = low[9:10, :]
    old_in = low[11:12, :] + 256.0 * high[11:12, :]
    weight = jnp.where(iota((LISTS, GROUP), 0).astype(F32) == old_in, scale, 0.0).astype(BF16)
    delta_acc[...] = dot(weight, x)
    pqk[0:8, 0:GROUP] = low[0:8, :]
    pqk[8:16, 0:GROUP] = high[0:8, :]
    lane_sub = iota((KSUB, 128), 1) // 16
    code = iota((KSUB, GROUP), 0).astype(F32).astype(BF16)
    scale_b = jnp.broadcast_to(scale.astype(BF16), (KSUB, GROUP))
    none = jnp.zeros((), BF16)

    def code_sums(hits_of, half, cols, dims):
        total = jnp.zeros((KSUB, 128), F32)
        for first in range(0, 8, STACK):
            these = range(first, first + STACK)
            hits = [hits_of((i // 4) * 8 + half * 4 + i % 4) for i in these]
            sums = dot(jnp.concatenate(hits, axis=0), cols, dims)
            for at, i in enumerate(these):
                own = lane_sub == 2 * (i % 4) + i // 4
                total = jnp.where(own, sums[at * KSUB : (at + 1) * KSUB, :], total)
        return total

    for half in range(2):
        cols = x[:, half * 128 : (half + 1) * 128]

        def value_hits(row):
            return jnp.where(code == pqk[row : row + 1, 0:GROUP].astype(BF16), scale_b, none)

        book[half * KSUB : (half + 1) * KSUB, :] = code_sums(value_hits, half, cols, NN)

    cent_copy.wait()
    eye = jnp.where(iota((COLS, COLS), 0) == iota((COLS, COLS), 1), 1.0, 0.0).astype(BF16)
    cent_t = dot(eye, cent[...], NT).astype(BF16)

    code = iota((KSUB, HALF * SLOTS), 0).astype(F32).astype(BF16)
    one = jnp.ones((), BF16)

    def unpack(part):
        held = erecv[part * HALF : (part + 1) * HALF].reshape(HALF, SLOTS * KK)
        held = jnp.concatenate([held, pltpu.roll(held, SLOTS * KK - KK, 1)], axis=0)
        got = jnp.transpose(held)
        new_rows = []
        scale_rows = []
        for q in range(0, SLOTS, 2):
            pairs = got[q * KK : q * KK + 8, :]
            odd = jnp.floor(pairs * (1.0 / 256.0))
            at = part * HALF * SLOTS + q * HALF
            pqk[0:8, at : at + 128] = pairs - 256.0 * odd
            pqk[8:16, at : at + 128] = odd
            new_rows.append(got[q * KK + 8 : q * KK + 9, :])
            scale_rows.append(got[q * KK + 9 : q * KK + 10, :])
        new_in = jnp.concatenate(new_rows, axis=1) - 1.0
        inside = iota((LISTS, HALF * SLOTS), 0).astype(F32) == new_in
        centg[part] = dot(cent_t, jnp.where(inside, 1.0, 0.0).astype(BF16)).astype(BF16)
        return inside, jnp.concatenate(scale_rows, axis=1)

    def cent_sums(part, half):
        lanes = slice(part * HALF * SLOTS, (part + 1) * HALF * SLOTS)

        def cent_hits(row):
            return jnp.where(code == pqk[row : row + 1, lanes].astype(BF16), one, none)

        return code_sums(cent_hits, half, centg[part, half * 128 : (half + 1) * 128, :], NT)

    most = erecv.at[pl.ds(0, HALF - 1)]
    copy_to(most, most, es_sem, er_sem.at[0], lists=sibling).wait_recv()
    near_inside, near_scale = unpack(0)
    for half in range(2):
        at = slice(half * KSUB, (half + 1) * KSUB)
        book[at, :] = book[at, :] - cent_sums(0, half)
    send_vecs(V1, V2)
    most = erecv.at[pl.ds(HALF, HALF)]
    copy_to(most, most, es_sem, er_sem.at[1], lists=sibling).wait_recv()
    far_inside, far_scale = unpack(1)
    pairs = []
    for half in range(2):
        total = cent_sums(1, half)
        part = pl.ds(half * 16, 16)
        comb[part] = (book[half * KSUB : (half + 1) * KSUB, :] - total).reshape(16, 2, 8, 128)
        pair = copy_to(
            comb.at[part, 1 - core], sib.at[part], bs_sem.at[half], br_sem.at[half], lists=sibling
        )
        pair.start()
        pairs.append(pair)

    block = z // 4

    def send_tiles(half):
        def send_tile(dy, near):
            row = wrap(y + dy, 8)
            place = 2 * lax.rem(row + half, 2) + core
            ahead = wrap(place - z + 8, 8)
            close = (ahead <= 2) | (ahead >= 6)
            col = jnp.where(close, 1 - near, near)
            there = row * 8 + 4 * col + place

            @pl.when(there != chip)
            def _():
                copy_to(
                    sib.at[half * 16 + row * 2 + col],
                    rsbuf.at[chip],
                    rs_sem,
                    rr_sem,
                    lists=2 * there + core,
                ).start()

        far_first = [(dy, near) for dy in range(8) for near in range(2)]
        for dy, near in sorted(far_first, key=lambda d: 2 * d[1] - hops(d[0])):
            send_tile(dy, near)

    for half in range(2):
        part = pl.ds(half * 16, 16)
        pairs[half].wait()
        sib[part] = sib[part] + comb[part, core]
        send_tiles(half)
    send_vecs(V2, V3)
    mine = lax.rem(y + z // 2, 2) * 16 + y * 2 + block
    sums_here = lax.rem(z, 2) == core

    @pl.when(sums_here)
    def _():
        rsbuf[chip] = sib[mine]
        most = rsbuf.at[pl.ds(0, CHIPS - 1)]
        copy_to(most, most, rs_sem, rr_sem, lists=sibling).wait_recv()
        total = jnp.sum(rsbuf[...], axis=0)
        shift = lax.rem(iota((8, 128), 1) // 16 - iota((8, 128), 0) + 8, 8)
        turned = total
        for d in range(1, 8):
            moved = pltpu.roll(pltpu.roll(total, 8 - d, 0), 16 * d, 1)
            turned = jnp.where(shift == d, moved, turned)
        tile[...] = turned
        gathered[core, mine] = turned

        def send_sum(peer):
            copy_to(
                tile, gathered.at[core, mine], gs_sem, gr_sem.at[mine // 16], lists=peer
            ).start()

        for dy, dz in FAR_FIRST:
            send_sum(rows[dy] + places[dz] + core)

    most = erecv.at[pl.ds(0, N_LISTS - 1)]
    copy_to(most, most, es_sem, er_sem.at[0], lists=sibling).wait_send()

    most = vrecv.at[pl.ds(0, N_LISTS - 1)]
    wait = copy_to(most, most, vs_sem, vr_sem, lists=sibling)
    wait.wait_recv()
    wait.wait_send()
    vflat[...] = vrecv[...].astype(F32).reshape(N_LISTS * 16, 128)
    vecs = jnp.concatenate(
        [
            jnp.concatenate(
                [
                    vflat[pl.ds(part * HALF * 16 + h * 8 + q, HALF, stride=16), :].astype(BF16)
                    for h in range(2)
                ],
                axis=1,
            )
            for part in range(2)
            for q in range(SLOTS)
        ],
        axis=0,
    )
    weight = jnp.concatenate(
        [jnp.where(near_inside, near_scale, 0.0), jnp.where(far_inside, far_scale, 0.0)], axis=1
    ).astype(BF16)
    delta_out[...] = (dot(weight, vecs) - delta_acc[...]).astype(BF16)

    gives = []
    for half in range(2):
        own_half = sums_here & (mine // 16 == half)

        @pl.when(own_half)
        def _():
            most = gathered.at[core, pl.ds(0, 15)]
            copy_to(most, most, gs_sem, gr_sem.at[half], lists=sibling).wait_recv()

        @pl.when(jnp.logical_not(own_half))
        def _():
            most = gathered.at[core, pl.ds(0, 16)]
            copy_to(most, most, gs_sem, gr_sem.at[half], lists=sibling).wait_recv()

        part = gathered.at[core, pl.ds(half * 16, 16)]
        give = copy_to(part, part, ts_sem.at[half], tr_sem.at[half], lists=sibling)
        give.start()
        gives.append(give)

    @pl.when(sums_here)
    def _():
        most = rsbuf.at[pl.ds(0, CHIPS - 1)]
        copy_to(most, most, gs_sem, gr_sem, lists=sibling).wait_send()
        most = sib.at[pl.ds(0, CHIPS // 2 - 1)]
        copy_to(most, most, rs_sem, rr_sem, lists=sibling).wait_send()

    @pl.when(jnp.logical_not(sums_here))
    def _():
        copy_to(sib, sib, rs_sem, rr_sem, lists=sibling).wait_send()

    for give in gives:
        give.wait()
    for t in range(CHIPS):
        half, block = t // 32, t % 32
        book_out[half * 8 : half * 8 + 8, block * 128 : (block + 1) * 128] = gathered[
            t % 2, t // 2
        ]


def body(vector_codes, row_scales, old_list, new_list, pq_codes, centroids):
    vmem = pl.BlockSpec(memory_space=pltpu.VMEM)
    hbm = pl.BlockSpec(memory_space=pltpu.HBM)
    return pl.pallas_call(
        kernel,
        name="rebuild_window",
        out_shape=(
            pltpu.VMEM((LISTS, COLS), BF16),
            pltpu.VMEM((16, 4096), F32),
        ),
        in_specs=[hbm] * 6,
        out_specs=(vmem, vmem),
        scratch_shapes=[
            pltpu.VMEM((1, ROWS), BF16),
            pltpu.VMEM((1, ROWS), I32),
            pltpu.VMEM((1, ROWS), I32),
            pltpu.VMEM((64, ROWS), I32),
            pltpu.VMEM((LISTS, COLS), BF16),
            pltpu.VMEM((N_REP, ROWS, COLS), BF16),
            pltpu.VMEM((N_REP, 32, ROWS), BF16),
            pltpu.VMEM((N_REP, 32, ROWS), BF16),
            pltpu.VMEM((N_LISTS, 1, 128), F32),
            pltpu.VMEM((N_LISTS, 1, 128), F32),
            pltpu.VMEM((N_LISTS, 16, 128), BF16),
            pltpu.VMEM((N_LISTS, 16, 128), BF16),
            pltpu.VMEM((LISTS, COLS), F32),
            pltpu.VMEM((N_LISTS * 16, 128), F32),
            pltpu.VMEM((16, N_LISTS * SLOTS), F32),
            pltpu.VMEM((2, COLS, HALF * SLOTS), BF16),
            pltpu.VMEM((2 * KSUB, 128), F32),
            pltpu.VMEM((CHIPS // 2, 8, 128), F32),
            pltpu.VMEM((CHIPS // 2, 2, 8, 128), F32),
            pltpu.VMEM((CHIPS, 8, 128), F32),
            pltpu.VMEM((8, 128), F32),
            pltpu.VMEM((2, CHIPS // 2, 8, 128), F32),
        ]
        + [pltpu.SemaphoreType.DMA((3,))]
        + [pltpu.SemaphoreType.DMA] * 8
        + [pltpu.SemaphoreType.DMA((2,))]
        + [pltpu.SemaphoreType.DMA] * 2
        + [pltpu.SemaphoreType.DMA((2,))] * 2
        + [pltpu.SemaphoreType.DMA] * 2
        + [pltpu.SemaphoreType.DMA((2,))] * 2
        + [pltpu.SemaphoreType.DMA]
        + [pltpu.SemaphoreType.DMA((2,))]
        + [pltpu.SemaphoreType.REGULAR],
        compiler_params=pltpu.CompilerParams(
            collective_id=0, has_side_effects=True, vmem_limit_bytes=56 * 1024 * 1024
        ),
    )(
        vector_codes,
        row_scales.reshape(1, ROWS),
        old_list.reshape(1, ROWS),
        new_list.reshape(1, ROWS),
        pq_codes.T,
        centroids,
    )


def solution(mesh):
    return jax.shard_map(
        body,
        mesh=mesh,
        in_specs=(
            P(("lists", "rep"), None),
            P(("lists", "rep")),
            P(("lists", "rep")),
            P(("lists", "rep")),
            P(("lists", "rep"), None),
            P("lists", None),
        ),
        out_specs=(P("lists", "rep"), P("rep", None)),
        check_vma=False,
    )
```
